32 devices in a mesh: expert: 8 (over z, y), shard: 4 (over x, core).
Axes of the slice: x: 2, y: 2, z: 4, core: 2. Of those that a mesh axis runs over, the one named last changes fastest.
Arguments:
- residual_in: float32 [32768, 768], P(('expert', 'shard')), may hold values from -6 to 6
- norm1_gain: float32 [768], replicated, may hold values from 0.1 to 1.9
- w_projection: bfloat16 [768, 2304], P('shard'), may hold values from -0.21875 to 0.21875
- rel_bias: float32 [12, 32], replicated, may hold values from -3 to 3
- w_attn_out: bfloat16 [768, 768], P('shard'), may hold values from -0.625 to 0.625
- norm2_gain: float32 [768], replicated, may hold values from 0.1 to 1.9
- w_router: bfloat16 [768, 8], replicated, may hold values from -0.109375 to 0.109375
- expert_in: bfloat16 [8, 768, 3072], P('expert', None, 'shard'), may hold values from -0.21875 to 0.21875
- expert_out: bfloat16 [8, 3072, 768], P('expert', 'shard'), may hold values from -0.15625 to 0.15625
- segments: int32 [32, 1024], P(('expert', 'shard')), may hold values from 0 to 63, never falling along the last dimension, each value on 1 to 512 neighbouring positions
- routes: int32 [32768, 2], P(('expert', 'shard')), may hold values from 0 to 7, all different within a row; in each aligned block of 1024 rows (0 to 1023, 1024 to 2047, ...) at most 320 rows name the same one
- out_grad: float32 [32768, 768], P(('expert', 'shard')), may hold values from -6 to 6
Outputs:
- block_out: float32 [32768, 768], P(('expert', 'shard'))
- residual_grad: float32 [32768, 768], P(('expert', 'shard'))
- norm1_gain_grad: float32 [768], replicated
- projection_grad: float32 [768, 2304], P('shard')
- rel_bias_grad: float32 [12, 32], replicated
- attn_out_grad: float32 [768, 768], P('shard')
- norm2_gain_grad: float32 [768], replicated
- router_grad: float32 [768, 8], replicated
- expert_in_grad: float32 [8, 768, 3072], P('expert', None, 'shard')
- expert_out_grad: float32 [8, 3072, 768], P('expert', 'shard')
The draws below stay inside these ranges and needn't reach their ends.
Inputs may be any that keep to these rules, and one draw needn't show every extreme that they name: `segments`: along each sequence the numbers never fall; each document spans 1 to 512 positions, and one spans exactly that many. `routes`: each token names two different experts. Among the rows of one device no expert is named more than 320 times, and in every draw some expert is named exactly 320 times by the rows of some device.
All inputs are finite; a program needn't handle non-finite values.
Results may differ from the reference program's by a relative error of at most 0.017.
Values may be sent and summed in bfloat16 or wider, within the bound.
A program may use at most 448 MiB of HBM per device.

```python
import math
import jax
import jax.numpy as jnp
import numpy as np
from jax import lax

D = 768
HEADS = 12
HEAD_DIM = 64
FF = 3072
BUCKETS = 32
SEQ = 1024
EXPERTS = 8
TOK_DEV = 1024
SEQS = 32
TOKENS = 32768
CAP = 320
DEVICES = 32


def block_scale(rng, dims, cuts, least, high):
    loudness = 1.0
    for dim, blocks in cuts:
        heights = jax.random.uniform(jax.random.fold_in(jax.random.fold_in(rng, 6), dim), (blocks,), jnp.float32, least / len(cuts), high / len(cuts))
        loudness = loudness * jnp.repeat(jnp.exp(heights), dims[dim] // blocks).reshape((-1,) + (1,) * (len(dims) - 1 - dim))
    return loudness


def split_up(amount, total, reach, slope):
    weights = [(1 << 20) // math.isqrt(standing ** slope) + 1 for standing in range(2, amount + 1)]
    spare, counts = total - reach - (amount - 1), [1] * (amount - 1)
    while spare > 0:
        free = [i for i in range(amount - 1) if counts[i] < reach]
        mass, budget = sum([weights[i] for i in free]), spare
        for i in free:
            extra = min(reach - counts[i], max(1, budget * weights[i] // mass), spare)
            counts[i] = counts[i] + extra
            spare = spare - extra
    return np.array([reach] + counts)


def ragged(rng, number_of, total, reach, slope):
    if number_of == 2:
        one = jax.random.randint(rng, (), max(1, total - reach), min(reach, total - 1) + 1)
        return jnp.stack([one, total - one])
    lengths = jnp.asarray(split_up(number_of, total, reach, slope), jnp.int32)
    pairs = (number_of - 1) // 2
    source_of, sink = lengths[1:1 + 2 * pairs:2], lengths[2:2 + 2 * pairs:2]
    margin = jnp.minimum(source_of - 1, reach - sink)
    passed = jax.random.randint(jax.random.fold_in(rng, 1), (pairs,), 0, 1 << 20) % (margin + 1)
    lengths = lengths.at[1:1 + 2 * pairs:2].set(source_of - passed).at[2:2 + 2 * pairs:2].set(sink + passed)
    return lengths[jax.random.permutation(jax.random.fold_in(rng, 2), number_of)]


def deal_out(rng, own, number, rows, count, top, most, slope):
    sequence = jax.random.permutation(rng, count)
    packed, common = portions_of(count, rows * top, most, slope, True), portions_of(count, rows * top, most, slope, False)
    places = jnp.arange(count)

    def named(lengths, turn):
        used = int((lengths > 0).sum())
        fixed = max(1, used // 4)
        moved = fixed + (places - fixed + turn * (used - fixed)) % max(1, count - fixed)
        return jnp.zeros((count,), jnp.int32).at[sequence[jnp.where(places < fixed, places, moved)]].set(jnp.asarray(lengths, jnp.int32))

    lengths = jnp.where(number % 4 == 0, named(packed, number // 4), named(common, number - number // 4 - 1))
    mixed = jax.random.permutation(jax.random.fold_in(own, 3), count)
    donor, taker = mixed[0:count // 2 * 2:2], mixed[1:count // 2 * 2:2]
    margin = jnp.minimum(lengths[donor] - 1, most - lengths[taker]) // 2
    margin = jnp.where((donor == sequence[0]) | (taker == sequence[0]) | (lengths[taker] == 0), 0, jnp.maximum(margin, 0))
    moved = jax.random.randint(jax.random.fold_in(own, 4), (count // 2,), 0, 1 << 20) % (margin + 1)
    lengths = lengths.at[donor].add(-moved).at[taker].add(moved)
    members = jnp.searchsorted(jnp.cumsum(lengths), jnp.arange(rows * top), side="right").astype(jnp.int32)
    grid = members.reshape(top, rows).T
    grid = grid[jax.random.permutation(jax.random.fold_in(own, 1), rows)]
    turn = jax.random.randint(jax.random.fold_in(own, 2), (rows, 1), 0, top)
    return jnp.take_along_axis(grid, (jnp.arange(top)[None, :] + turn) % top, axis=1)


def portions_of(count, total, reach, skew, full):
    loads = [(1 << 20) // math.isqrt(rank ** skew) + 1 for rank in range(1, count + 1)]
    largest = reach if full else min(reach, max(-(-total // count), total * loads[0] // sum(loads)))
    least = 1 if total - largest >= count - 1 else 0
    holding, spare = [largest] + [least] * (count - 1), total - largest - least * (count - 1)
    while spare > 0:
        candidates = [i for i in range(1, count) if holding[i] < largest] or [i for i in range(1, count) if holding[i] < reach]
        pool, budget = sum([loads[i] for i in candidates]), spare
        for i in candidates:
            more = min(reach - holding[i], max(1, budget * loads[i] // pool), spare)
            holding[i] = holding[i] + more
            spare = spare - more
    return np.array(holding)


def bell_draw(rng, extent, width, limit, cuts=(), kind=jnp.bfloat16):
    drawn = jax.random.normal(rng, extent, jnp.float32) * width
    if len(cuts) > 0:
        drawn = block_scale(rng, extent, cuts, -0.22, 0.18) * drawn
    return jnp.clip(drawn, min=-limit, max=limit).astype(kind)


def setup_inputs(seed: int = 0) -> dict:
    splits = jax.random.split(jax.random.key(seed), 13)
    residual_in = bell_draw(splits[0], (TOKENS, D), 1.0, 6.0, ((0, 32),), jnp.float32)
    norm1_gain = jnp.clip(1.0 + 0.18 * jax.random.normal(splits[1], (D,), jnp.float32), 0.1, 1.9)
    w_projection = bell_draw(splits[2], (D, 3 * D), D ** -0.5, 0.21875, ((0, 4),))
    rel_bias = bell_draw(splits[3], (HEADS, BUCKETS), 0.5, 3.0, (), jnp.float32)
    w_attn_out = bell_draw(splits[4], (D, D), (D // 8) ** -0.5, 0.625, ((0, 4),))
    norm2_gain = jnp.clip(1.0 + 0.18 * jax.random.normal(splits[5], (D,), jnp.float32), 0.1, 1.9)
    w_router = bell_draw(splits[6], (D, EXPERTS), (4 * D) ** -0.5, 0.109375)
    expert_in = bell_draw(splits[7], (EXPERTS, D, FF), D ** -0.5, 0.21875, ((0, 8), (2, 4)))
    expert_out = bell_draw(splits[8], (EXPERTS, FF, D), (FF // 2) ** -0.5, 0.15625, ((0, 8), (1, 4)))
    segments = jax.vmap(lambda own: jnp.searchsorted(jnp.cumsum(ragged(own, max(4, SEQ // 16), SEQ, SEQ // 2, 2)), jnp.arange(SEQ), side="right"))(jax.random.split(splits[9], SEQS)).reshape((SEQS, SEQ)).astype(jnp.int32)
    routes_keys = jax.random.split(jax.random.fold_in(splits[10], 1), TOKENS // TOK_DEV)
    routes_turns = jax.random.permutation(jax.random.fold_in(splits[10], 3), TOKENS // TOK_DEV)
    routes = jax.vmap(lambda own, number: deal_out(jax.random.fold_in(splits[10], 2), own, number, TOK_DEV, EXPERTS, 2, CAP, 2))(routes_keys, routes_turns).reshape((TOKENS, 2))
    out_grad = bell_draw(splits[11], (TOKENS, D), 1.0, 6.0, ((0, 32),), jnp.float32)
    return dict(residual_in=residual_in, norm1_gain=norm1_gain, w_projection=w_projection, rel_bias=rel_bias, w_attn_out=w_attn_out, norm2_gain=norm2_gain, w_router=w_router, expert_in=expert_in, expert_out=expert_out, segments=segments, routes=routes, out_grad=out_grad)


epsilon = 1e-06
bucket_borders = (19, 21, 24, 27, 31, 35, 40, 46, 52, 59, 67, 77, 87, 99, 113)

@jax.custom_vjp
def low(v):
    return lax.optimization_barrier(v.astype(jnp.bfloat16)).astype(jnp.float32)

@jax.custom_vjp
def low_back(v):
    return v

def low_keep(v):
    return (low(v), None)

def low_pass(kept, grad):
    return (grad,)

def back_keep(v):
    return (v, None)

def back_low(kept, grad):
    return (low(grad),)
low.defvjp(low_keep, low_pass)
low_back.defvjp(back_keep, back_low)

def bucket_of(distance):
    beyond = jnp.zeros_like(distance)
    for border in bucket_borders:
        beyond = beyond + (distance >= border).astype(jnp.int32)
    return jnp.where(distance < 16, distance, 16 + beyond)

def rms_scale(values):
    return lax.rsqrt(lax.optimization_barrier(jnp.mean(values * values, axis=-1, keepdims=True)) + epsilon)

def dispatch_tables(routes):
    flat = routes.reshape(DEVICES, 2 * TOK_DEV).astype(jnp.int32)
    member = (flat[:, :, None] == jnp.arange(EXPERTS, dtype=jnp.int32)[None, None, :]).astype(jnp.int32)
    earlier = jnp.cumsum(member, axis=1) - member
    position = lax.optimization_barrier(jnp.sum(earlier * member, axis=2))
    place = flat * (DEVICES * CAP) + jnp.arange(DEVICES, dtype=jnp.int32)[:, None] * CAP + position
    place = place.reshape(-1).astype(jnp.int32)
    owner = jnp.full((EXPERTS * DEVICES * CAP,), 2 * TOKENS, jnp.int32)
    owner = owner.at[place].set(jnp.arange(2 * TOKENS, dtype=jnp.int32))
    return (owner, place)

def layer(residual_in, norm1_gain, w_projection, rel_bias, w_attn_out, norm2_gain, w_router, expert_in, expert_out, segments, routes, owner, place):
    highest = lax.Precision.HIGHEST
    normed = low(residual_in * rms_scale(residual_in) * norm1_gain)
    projected = low(low_back(jnp.dot(normed, w_projection, precision=highest)))
    split = projected.reshape(SEQS, SEQ, 3, HEADS, HEAD_DIM)
    distance = jnp.arange(SEQ, dtype=jnp.int32)[:, None] - jnp.arange(SEQ, dtype=jnp.int32)[None, :]
    bias_full = rel_bias[:, bucket_of(jnp.maximum(distance, 0))]
    scale = HEAD_DIM ** (-0.5)

    def attend(pieces):
        block, marks = pieces
        scores = jnp.einsum('qhd,khd->hqk', block[:, 0], block[:, 1], precision=highest) * scale + bias_full
        scores = low_back(scores)
        allowed = (distance >= 0) & (marks[:, None] == marks[None, :])
        shares = low(jax.nn.softmax(jnp.where(allowed[None], scores, -1e+30), axis=-1))
        return jnp.einsum('hqk,khd->qhd', shares, block[:, 2], precision=highest)
    mixed = lax.map(jax.checkpoint(attend), (split, segments))
    merged = low(low_back(mixed.reshape(TOKENS, D)))
    hidden = residual_in + low_back(jnp.dot(merged, w_attn_out, precision=highest))
    normed2 = low(hidden * rms_scale(hidden) * norm2_gain)
    logits = jnp.dot(normed2, w_router, precision=highest)
    gates = jax.nn.softmax(jnp.take_along_axis(logits, routes, axis=1), axis=-1)
    padded = jnp.concatenate([normed2, jnp.zeros((1, D), normed2.dtype)], axis=0)
    rows = low_back(padded[owner // 2]).reshape(EXPERTS, DEVICES * CAP, D)

    def expert(pieces):
        block, inner, outer = pieces
        before_gelu = low_back(jnp.dot(block, inner, precision=highest))
        active = low(jax.nn.gelu(before_gelu))
        return low(low_back(jnp.dot(active, outer, precision=highest)))
    produced = lax.map(jax.checkpoint(expert), (rows, expert_in, expert_out)).reshape(-1, D)
    paired = produced[place].reshape(TOKENS, 2, D)
    return hidden + lax.optimization_barrier(jnp.sum(gates[:, :, None] * paired, axis=1))

def reference(residual_in, norm1_gain, w_projection, rel_bias, w_attn_out, norm2_gain, w_router, expert_in, expert_out, segments, routes, out_grad):
    owner, place = dispatch_tables(routes)

    def forward(a, b, c, d, e, f, g, h, i):
        return layer(a, b, c, d, e, f, g, h, i, segments, routes, owner, place)
    primals = (residual_in, norm1_gain, w_projection.astype(jnp.float32), rel_bias, w_attn_out.astype(jnp.float32), norm2_gain, w_router.astype(jnp.float32), expert_in.astype(jnp.float32), expert_out.astype(jnp.float32))
    block_out, pullback = jax.vjp(forward, *primals)
    grads = pullback(out_grad)
    return (block_out, grads[0], grads[1], grads[2], grads[3], grads[4], grads[5], grads[6], grads[7], grads[8])
```

```python
import functools

import jax
import jax.numpy as jnp
import numpy as np
from jax import lax
from jax.experimental import pallas as pl
from jax.experimental.pallas import tpu as pltpu
from jax.sharding import PartitionSpec as P

bucket_borders = (19, 21, 24, 27, 31, 35, 40, 46, 52, 59, 67, 77, 87, 99, 113)
longest = 512
tile = 256
span = 3 * tile
lanes = 128
masked = -1e30
f32 = jnp.float32
bf16 = jnp.bfloat16


def one_hot_buckets(distance, buckets):
    distance = np.clip(distance, 0, None)
    beyond = sum((distance >= border).astype(np.int32) for border in bucket_borders)
    bucket = np.where(distance < 16, distance, 16 + beyond)
    return (bucket[:, None] == np.arange(buckets)[None, :]).astype(np.float32)


def bias_tables(buckets):
    lane = np.arange(span)
    rows = np.where(lane < 2 * tile, tile - lane, tile + span - lane)
    turned = np.where(lane < tile, tile + lane, tile + lane - span)
    return (one_hot_buckets(rows, buckets), one_hot_buckets(turned, buckets))


def key_start(first):
    return max(0, first - longest) // tile * tile


def dot_nt(a, b):
    return lax.dot_general(a, b, (((1,), (1,)), ((), ())), preferred_element_type=f32)


def dot_tn(a, b):
    return lax.dot_general(a, b, (((0,), (0,)), ((), ())), preferred_element_type=f32)


def dot_nn(a, b):
    return lax.dot_general(a, b, (((1,), (0,)), ((), ())), preferred_element_type=f32)


def attend_forward_pair(
    head_dim, pair, q_ref, k_ref, v_ref, base_ref, out_ref, log_ref, mask_ref
):
    seq_len = q_ref.shape[0]
    scale = head_dim ** (-0.5)
    per_pair = lanes // head_dim
    lane = lax.broadcasted_iota(jnp.int32, (tile, lanes), 1)
    tables = []
    for head in range(per_pair):
        wide = jnp.broadcast_to(base_ref[head : head + 1, :], (tile, span))
        tables.append(pltpu.roll(wide, 0, 1, stride=1, stride_axis=0))
    for first in range(0, seq_len, tile):
        start = key_start(first)
        merged = jnp.zeros((tile, lanes), f32)
        logs = log_ref[first : first + tile, :]
        for head in range(per_pair):
            inside = (lane >= head * head_dim) & (lane < (head + 1) * head_dim)
            query = jnp.where(inside, q_ref[first : first + tile, :] * scale, 0.0).astype(bf16)
            pieces = []
            for begin in range(start, first + tile, tile):
                piece = dot_nt(query, k_ref[begin : begin + tile, :])
                back = (first - begin) // tile
                if back == 0:
                    piece = piece + tables[head][:, tile : 2 * tile]
                elif back == 1:
                    piece = piece + tables[head][:, :tile]
                else:
                    piece = piece + base_ref[head : head + 1, :1]
                place = begin - start
                pieces.append(piece + mask_ref[first : first + tile, place : place + tile])
            peak = functools.reduce(jnp.maximum, pieces)
            peak = jnp.max(peak, axis=1, keepdims=True)
            weights = [jnp.exp(piece - peak) for piece in pieces]
            total = jnp.sum(functools.reduce(jnp.add, weights), axis=1, keepdims=True)
            mixed = jnp.zeros((tile, lanes), f32)
            for index, weight in enumerate(weights):
                begin = start + index * tile
                mixed = mixed + dot_nn(weight.astype(bf16), v_ref[begin : begin + tile, :])
            merged = jnp.where(inside, mixed * (1.0 / total), merged)
            logs = jnp.where(lane == pair * per_pair + head, peak + jnp.log(total), logs)
        out_ref[first : first + tile, :] = merged.astype(bf16)
        log_ref[first : first + tile, :] = logs


def attend_backward_pair(
    head_dim,
    pair,
    q_ref,
    k_ref,
    v_ref,
    grad_ref,
    base_ref,
    dq_ref,
    dk_ref,
    dv_ref,
    bias_ref,
    mask_ref,
    log_turned,
    dk_total,
    dv_total,
    diagonal,
):
    seq_len = q_ref.shape[0]
    scale = head_dim ** (-0.5)
    per_pair = lanes // head_dim
    firsts = range(0, seq_len, tile)
    dk_total[...] = jnp.zeros_like(dk_total)
    dv_total[...] = jnp.zeros_like(dv_total)
    lane = lax.broadcasted_iota(jnp.int32, (tile, lanes), 1)
    tables = []
    for head in range(per_pair):
        wide = jnp.broadcast_to(base_ref[head : head + 1, :], (2 * tile, span))
        tables.append(pltpu.roll(wide, 0, 1, stride=1, stride_axis=0)[:, :tile])
    diagonal[...] = jnp.zeros_like(diagonal)
    far = [jnp.zeros((1, tile), f32) for _ in range(per_pair)]
    for first in firsts:
        start = key_start(first)
        query_grad = jnp.zeros((tile, lanes), f32)
        for head in range(per_pair):
            inside = (lane >= head * head_dim) & (lane < (head + 1) * head_dim)

            def own(values):
                return jnp.where(inside, values, 0.0).astype(bf16)

            query = own(q_ref[first : first + tile, :] * scale)
            grad = own(grad_ref[first : first + tile, :])
            row = log_turned[pl.ds(pair * per_pair + head, 1), first : first + tile]
            begins = range(start, first + tile, tile)
            shares, dots = [], []
            inner = jnp.zeros((1, tile), f32)
            for begin in begins:
                piece = dot_nt(k_ref[begin : begin + tile, :], query)
                back = (first - begin) // tile
                if back == 0:
                    piece = piece + tables[head][tile:, :]
                elif back == 1:
                    piece = piece + tables[head][:tile, :]
                else:
                    piece = piece + base_ref[head : head + 1, :1]
                place = begin - start
                piece = piece + mask_ref[place : place + tile, first : first + tile]
                share = jnp.exp(piece - row)
                dot = dot_nt(v_ref[begin : begin + tile, :], grad)
                inner = inner + jnp.sum(share * dot, axis=0, keepdims=True)
                dv_total[begin : begin + tile, :] += dot_nn(share.astype(bf16), grad)
                shares.append(share)
                dots.append(dot)
            for begin, share, dot in zip(begins, shares, dots):
                back = (first - begin) // tile
                score_grad = share * (dot - inner)
                if back < 2:
                    top = (1 - back) * tile
                    diagonal[head, top : top + tile, :tile] += score_grad
                else:
                    far[head] = far[head] + jnp.sum(score_grad, axis=0, keepdims=True)
                score_grad = score_grad.astype(bf16)
                dk_total[begin : begin + tile, :] += dot_nn(score_grad, query)
                query_grad = query_grad + dot_tn(
                    score_grad, own(k_ref[begin : begin + tile, :] * scale)
                )
        dq_ref[first : first + tile, :] = query_grad.astype(bf16)
    dk_ref[...] = dk_total[...].astype(bf16)
    dv_ref[...] = dv_total[...].astype(bf16)
    for head in range(per_pair):
        grouped = diagonal[head, :8, :]
        for top in range(8, 2 * tile, 8):
            grouped = grouped + pltpu.roll(diagonal[head, top : top + 8, :], span - top, 1)
        sums = grouped[:1, :]
        for row in range(1, 8):
            sums = sums + pltpu.roll(grouped[row : row + 1, :], span - row, 1)
        bias_ref[head : head + 1, :tile] = sums[:, :tile] + far[head]
        bias_ref[head : head + 1, tile:] = sums[:, tile:]


hidden_tile = 768
block_count = 4
epsilon = 1e-06
mesh_ids = pl.DeviceIdType.MESH


def gelu_parts(values):
    factor = 0.7978845608028654
    squares = values * values
    turned = jnp.tanh(values * (factor + (factor * 0.044715) * squares))
    share = 0.5 + 0.5 * turned
    active = values * share
    inside = 2.0 * factor + (6.0 * factor * 0.044715) * squares
    return (active, share + active * ((1.0 - share) * inside))


def turned_row(row):
    return jnp.broadcast_to(row.astype(f32), (lanes, row.shape[1])).T


def split_digits(row):
    places = lax.broadcasted_iota(jnp.int32, (8, row.shape[1]), 0)
    digits = jnp.zeros(places.shape, f32)
    for place in range(3):
        digit = row.astype(bf16).astype(f32)
        digits = jnp.where(places == place, digit, digits)
        row = row - digit
    return digits.astype(bf16)


def paired(place, step, members):
    partner, bit = 0, 1
    while bit < members:
        ours, theirs = place // bit % 2, step // bit % 2
        partner = partner + bit * (ours + theirs - 2 * ours * theirs)
        bit = 2 * bit
    return partner


def group_place(members, shards):
    expert, shard = lax.axis_index("expert"), lax.axis_index("shard")
    half, side = members // 2, shards // 2

    def device_of(member):
        return {
            "expert": expert // half * half + lax.rem(member, half),
            "shard": member // half * side + lax.rem(shard, side),
        }

    return shard // side * half + lax.rem(expert, half), device_of


def add_remote(source, target, send, arrive, device):
    return pltpu.make_async_remote_copy(
        src_ref=source,
        dst_ref=target,
        send_sem=send,
        recv_sem=arrive,
        device_id=device,
        device_id_type=mesh_ids,
    )


def expert_kernel(
    shards,
    sent_ref,
    gates_ref,
    grads_ref,
    inner_ref,
    outer_ref,
    gated_out,
    back_out,
    gates_out,
    active_out,
    pre_out,
    inner_mine,
    outer_mine,
    outer_given,
    inner_crossed,
    inner_distant,
    rows,
    grads_held,
    scaled,
    actives,
    pres,
    gates_in,
    gates_back,
    value_total,
    row_total,
    inner_held,
    outer_held,
    turned,
    near_in,
    send_sems,
    arrive_sems,
    back_sems,
    returned_sems,
    gate_send,
    gate_arrive,
    digit_sems,
    digit_arrive,
    load_sems,
    weight_sems,
    active_sems,
    pre_sems,
    tile_sems,
    keep_sems,
    near_send,
    near_arrive,
    across_sems,
    distant_sems,
):
    members, capacity, _ = sent_ref.shape
    blocks, block, width = rows.shape
    units = actives.shape[2]
    quarters = actives.shape[1] // block
    block_steps = members // blocks
    me, device_of = group_place(members, shards)
    shard = lax.axis_index("shard")
    side = shards // 2
    low, turn = lax.rem(shard, side), shard // side
    far_low = lax.rem(low + 1, side)
    across = {"shard": lax.rem(shard + side, shards)}
    near = {"shard": turn * side + far_low}
    expert, half = lax.axis_index("expert"), members // 2
    native_here = expert // half == turn
    distant = {"expert": lax.rem(expert + half, members)}

    def source(step):
        return paired(me, step, members)

    def device(step):
        return device_of(source(step))

    def place_of(ref, step):
        start = pl.multiple_of(lax.rem(step, block_steps) * capacity, 16)
        return ref.at[step // block_steps, pl.ds(start, capacity)]

    def sending(step):
        return add_remote(
            sent_ref.at[source(step)],
            place_of(rows, step),
            send_sems.at[step],
            arrive_sems.at[step],
            device(step),
        )

    def sending_gates(step):
        return add_remote(
            gates_ref.at[source(step)],
            gates_in.at[step],
            gate_send.at[step],
            gate_arrive.at[step],
            device(step),
        )

    def returning(step):
        return add_remote(
            place_of(rows, step),
            back_out.at[me],
            back_sems.at[step],
            returned_sems.at[step],
            device(step),
        )

    def returning_gates(step):
        return add_remote(
            gates_back.at[step],
            gates_out.at[me],
            digit_sems.at[step],
            digit_arrive.at[step],
            device(step),
        )

    def loading(step):
        return pltpu.make_async_copy(
            grads_ref.at[source(step)], place_of(grads_held, step), load_sems.at[step]
        )

    def giving(step):
        return pltpu.make_async_copy(
            place_of(grads_held, step), gated_out.at[source(step)], load_sems.at[step]
        )

    def keeping(index, slot):
        return (
            pltpu.make_async_copy(actives.at[slot], active_out.at[index], active_sems.at[slot]),
            pltpu.make_async_copy(pres.at[slot], pre_out.at[index], pre_sems.at[slot]),
        )

    own_rows = pltpu.make_async_copy(sent_ref.at[me], place_of(rows, 0), arrive_sems.at[0])
    own_back = pltpu.make_async_copy(place_of(rows, 0), back_out.at[me], back_sems.at[0])
    own_digits = pltpu.make_async_copy(gates_back.at[0], gates_out.at[me], digit_sems.at[0])
    own_gates = pltpu.make_async_copy(gates_ref.at[me], gates_in.at[0], gate_arrive.at[0])
    weight_loads = (
        pltpu.make_async_copy(inner_ref, inner_held, weight_sems.at[0]),
        pltpu.make_async_copy(outer_ref, outer_held, weight_sems.at[1]),
    )
    barrier = pltpu.get_barrier_semaphore()
    for partner in (near, distant):
        pl.semaphore_signal(barrier, inc=1, device_id=partner, device_id_type=mesh_ids)

    @pl.loop(1, members)
    def _(step):
        pl.semaphore_signal(barrier, inc=1, device_id=device(step), device_id_type=mesh_ids)

    own_rows.start()
    own_gates.start()
    for copy in weight_loads:
        copy.start()

    @pl.loop(0, members)
    def _(step):
        loading(step).start()

    pl.semaphore_wait(barrier, members + 1)

    @pl.loop(1, members)
    def _(step):
        sending_gates(step).start()
        sending(step).start()

    for copy in weight_loads:
        copy.wait()
    own_rows.wait()
    own_gates.wait()

    @pl.loop(0, blocks)
    def _(index):
        slot = lax.rem(index, 2)

        @pl.loop(0, block_steps)
        def _(place):
            step = index * block_steps + place

            @pl.when(step > 0)
            def _():
                sending_gates(step).wait_recv()
                sending(step).wait_recv()

            loading(step).wait()

        @pl.when(index > 1)
        def _():
            for copy in keeping(index - 2, slot):
                copy.wait()

        gates = jnp.concatenate(
            [
                turned_row(gates_in[index * block_steps + place, :1, :])[:capacity, :1]
                for place in range(block_steps)
            ],
            axis=0,
        )
        scaled[...] = (gates * grads_held[index].astype(f32)).astype(bf16)
        held_columns = pl.ds(pl.multiple_of(index * block, lanes), block)
        turned[0, :, held_columns] = rows[index].T
        turned[1, :, held_columns] = scaled[...].T
        value_total[...] = jnp.zeros_like(value_total)
        row_total[...] = jnp.zeros_like(row_total)

        def units_of(part):
            return pl.ds(pl.multiple_of(part * units, units), units)

        def block_of(part):
            return pl.ds(pl.multiple_of(part * block, 16), block)

        def begin_part(part):
            active, slope = gelu_parts(dot_nn(rows[index], inner_held[:, units_of(part)]))
            actives[slot, block_of(part), :] = active.astype(bf16)
            pre = dot_nt(scaled[...], outer_held[units_of(part), :]) * slope
            pres[slot, block_of(part), :] = pre.astype(bf16)

        def end_part(part):
            value_total[...] += dot_nn(actives[slot, block_of(part), :], outer_held[units_of(part), :])
            row_total[...] += dot_nt(pres[slot, block_of(part), :], inner_held[:, units_of(part)])

        begin_part(0)

        @pl.loop(1, quarters)
        def _(part):
            end_part(part - 1)
            begin_part(part)

        end_part(quarters - 1)
        for copy in keeping(index, slot):
            copy.start()
        produced = value_total[...]
        rows[index] = row_total[...].astype(bf16)
        rest = jnp.sum(grads_held[index].astype(f32) * produced, axis=1, keepdims=True)
        grads_held[index] = (gates * produced).astype(bf16)
        spare = gates_back.shape[2] - capacity
        for place in range(block_steps):
            wide = jnp.broadcast_to(
                rest[place * capacity : (place + 1) * capacity, :], (capacity, lanes)
            )
            wide = jnp.concatenate([wide, jnp.zeros((spare, lanes), f32)], axis=0)
            gates_back[index * block_steps + place] = wide.T[:8, :]

        @pl.loop(0, block_steps)
        def _(place):
            step = index * block_steps + place
            giving(step).start()

            @pl.when(step > 0)
            def _():
                returning(step).start()
                returning_gates(step).start()

            @pl.when(step == 0)
            def _():
                own_back.start()
                own_digits.start()

    held_parts = (inner_held, outer_held)
    targets = {(0, 3): inner_mine, (1, 3): outer_mine, (1, 2): outer_given}
    places = (2 * far_low, 2 * far_low + 1, 2 * low + 1, 2 * low)
    order = [(matrix, position) for matrix in range(2) for position in range(4)]
    buffers = (actives.at[0], pres.at[0], actives.at[1], pres.at[1])

    def part_of(matrix, position):
        if matrix == 0:
            return inner_held.at[:, position * units : (position + 1) * units]
        return outer_held.at[position * width : (position + 1) * width, :]

    def tile_loads(count):
        matrix, position = order[count]
        kept = (pre_out, active_out)[matrix]
        start = pl.multiple_of(places[position] * block, 16)
        return [
            pltpu.make_async_copy(
                kept.at[index, pl.ds(start, block), :],
                buffers[count % 4].at[index * block : (index + 1) * block, :],
                tile_sems.at[count % 4, index],
            )
            for index in range(blocks)
        ]

    def near_copy(matrix, position):
        return add_remote(
            part_of(matrix, position),
            near_in.at[matrix, position],
            near_send.at[matrix, position],
            near_arrive.at[matrix, position],
            near,
        )

    lines_each = width // 4

    def lines_of(index):
        return slice(index * lines_each, (index + 1) * lines_each)

    def across_copy(index):
        return add_remote(
            part_of(0, 2).at[lines_of(index), :],
            inner_crossed.at[lines_of(index), :],
            across_sems.at[0, index],
            across_sems.at[1, index],
            across,
        )

    def distant_copy(index, source):
        return add_remote(
            source.at[lines_of(index), :],
            inner_distant.at[lines_of(index), :],
            distant_sems.at[0, index],
            distant_sems.at[1, index],
            distant,
        )

    def pass_on(index):
        @pl.when(native_here)
        def _():
            across_copy(index).wait_recv()
            distant_copy(index, inner_crossed).start()

    def keep_copy(matrix, position):
        index = {(0, 3): 0, (1, 3): 1, (1, 2): 2}[matrix, position]
        return pltpu.make_async_copy(
            part_of(matrix, position), targets[matrix, position], keep_sems.at[index]
        )

    for index in range(blocks - 2, blocks):
        for copy in keeping(index, index % 2):
            copy.wait()
    for count in range(4):
        for copy in tile_loads(count):
            copy.start()
    for count, (matrix, position) in enumerate(order):
        for copy in tile_loads(count):
            copy.wait()
        target = part_of(matrix, position)

        @pl.loop(0, units // tile)
        def _(part):
            columns = pl.ds(pl.multiple_of(part * tile, tile), tile)
            sums = dot_nn(turned[matrix], buffers[count % 4][:, columns])
            target[:, columns] = sums.astype(bf16)

        if count + 4 < len(order):
            for copy in tile_loads(count + 4):
                copy.start()
        if position < 2:
            near_copy(matrix, position).start()
        else:
            other = 3 - position
            near_copy(matrix, other).wait_recv()

            @pl.loop(0, width // tile)
            def _(part):
                lines = pl.ds(pl.multiple_of(part * tile, tile), tile)
                sums = target[lines, :].astype(f32) + near_in[matrix, other, lines, :].astype(f32)
                target[lines, :] = sums.astype(bf16)

            if (matrix, position) == (0, 2):
                for index in range(4):
                    across_copy(index).start()
            else:
                keep_copy(matrix, position).start()
            if (matrix, position) == (0, 3):

                @pl.when(jnp.logical_not(native_here))
                def _():
                    for index in range(2):
                        distant_copy(index, part_of(0, 3)).start()

        if count in (4, 6):
            pass_on((count - 4) // 2)

    own_back.wait()
    own_digits.wait()

    @pl.loop(1, members)
    def _(step):
        sending_gates(step).wait_send()
        sending(step).wait_send()
        returning(step).wait()
        returning_gates(step).wait()

    @pl.loop(0, members)
    def _(step):
        giving(step).wait()

    for matrix, position in targets:
        keep_copy(matrix, position).wait()
    @pl.when(jnp.logical_not(native_here))
    def _():
        for index in range(2):
            across_copy(index).wait_recv()

    for index in range(4):
        across_copy(index).wait_send()
        if index < 2:
            distant_copy(index, inner_crossed).wait()
        else:
            across_copy(index).wait_recv()
    for matrix in range(2):
        for position in range(2):
            near_copy(matrix, position).wait_send()


def run_experts(sent, gates, grads, inner, outer, shards):
    members, capacity, width = sent.shape
    hidden_units = inner.shape[1]
    units = hidden_units // shards
    blocks = block_count
    block = members // blocks * capacity
    anywhere = pl.BlockSpec(memory_space=pl.ANY)
    shape = jax.ShapeDtypeStruct
    hidden_shape = shape((blocks, shards * block, units), bf16)
    piece = shape((width, units), bf16)
    dma = pltpu.SemaphoreType.DMA
    outs = pl.pallas_call(
        functools.partial(expert_kernel, shards),
        in_specs=[anywhere] * 5,
        out_specs=[anywhere] * 10,
        out_shape=[
            shape((members, capacity, width), bf16),
            shape((members, capacity, width), bf16),
            shape(gates.shape, f32),
            hidden_shape,
            hidden_shape,
            piece,
            piece,
            piece,
            piece,
            shape((width // 2, units), bf16),
        ],
        scratch_shapes=[
            pltpu.VMEM((blocks, block, width), bf16),
            pltpu.VMEM((blocks, block, width), bf16),
            pltpu.VMEM((block, width), bf16),
            pltpu.VMEM((2, shards * block, units), bf16),
            pltpu.VMEM((2, shards * block, units), bf16),
            pltpu.VMEM(gates.shape, f32),
            pltpu.VMEM(gates.shape, f32),
            pltpu.VMEM((block, width), f32),
            pltpu.VMEM((block, width), f32),
            pltpu.VMEM((width, hidden_units), bf16),
            pltpu.VMEM((hidden_units, width), bf16),
            pltpu.VMEM((2, width, blocks * block), bf16),
            pltpu.VMEM((2, 2, width, units), bf16),
            dma((members,)),
            dma((members,)),
            dma((members,)),
            dma((members,)),
            dma((members,)),
            dma((members,)),
            dma((members,)),
            dma((members,)),
            dma((members,)),
            dma((2,)),
            dma((2,)),
            dma((2,)),
            dma((4, blocks)),
            dma((3,)),
            dma((2, 2)),
            dma((2, 2)),
            dma((2, 4)),
            dma((2, 2)),
        ],
        compiler_params=pltpu.CompilerParams(
            collective_id=0, has_side_effects=True, vmem_limit_bytes=63 * 2**20
        ),
        cost_estimate=pl.CostEstimate(
            flops=12 * members * capacity * width * hidden_units,
            bytes_accessed=2 * (members * capacity * (6 * width + 4 * hidden_units)),
            transcendentals=members * capacity * hidden_units,
        ),
    )(sent, gates, grads, inner, outer)
    return outs[:3] + outs[5:]


def front_kernel(
    shards,
    head_dim,
    residual_ref,
    gains_ref,
    projection_piece,
    attended_piece,
    inner_piece,
    outer_piece,
    route_rows,
    out_grad_ref,
    row_ref,
    base_ref,
    router_ref,
    projection_out,
    attended_out,
    projected_out,
    merged_out,
    logs_out,
    hidden_out,
    normed_out,
    normed2_out,
    counts_out,
    sent_out,
    gates_out,
    grads_out,
    inner_out,
    outer_out,
    projection_full,
    attended_full,
    projected,
    merged,
    logs,
    hidden,
    normed,
    normed2,
    counts,
    sent,
    gate_rows,
    sent_grads,
    low_grads,
    mask_ref,
    gate_table,
    given,
    out_sems,
    local_sems,
    shared_send,
    shared_arrive,
    grad_send,
    grad_arrive,
    distant_send,
    distant_arrive,
    across_send,
    across_arrive,
    near_send,
    near_arrive,
):
    tokens, width = residual_ref.shape
    members, capacity, _ = grads_out.shape
    expert, shard = lax.axis_index("expert"), lax.axis_index("shard")
    side, half = shards // 2, members // 2
    me, device_of = group_place(members, shards)
    low, turn = lax.rem(shard, side), shard // side
    native_here = expert // half == turn
    across = {"shard": lax.rem(shard + side, shards)}
    near = {"shard": turn * side + lax.rem(low + 1, side)}
    distant = {"expert": lax.rem(expert + half, members)}
    pieces = (inner_piece, outer_piece)
    units = outer_piece.shape[0]
    per_piece = 4
    chunk_rows = width // per_piece
    chunks = range(2 * per_piece)

    def piece(index):
        start = index % per_piece * chunk_rows
        return pieces[index // per_piece].at[start : start + chunk_rows, :]

    def slot(index, which):
        place = 2 * low + which
        start = index % per_piece * chunk_rows
        if index // per_piece == 0:
            columns = pl.ds(pl.multiple_of(place * units, units), units)
            return inner_out.at[start : start + chunk_rows, columns]
        return outer_out.at[pl.ds(pl.multiple_of(place * units + start, chunk_rows), chunk_rows), :]

    def passing(index):
        start = index % per_piece * chunk_rows
        return given.at[index // per_piece, start : start + chunk_rows, :]

    def distant_copy(index, target):
        return add_remote(
            piece(index), target, distant_send.at[index], distant_arrive.at[index], distant
        )

    def across_copy(index, source):
        return add_remote(
            source, slot(index, 1), across_send.at[index], across_arrive.at[index], across
        )

    def near_copy(index, which, source):
        return add_remote(
            source,
            slot(index, which),
            near_send.at[index, which],
            near_arrive.at[index, which],
            near,
        )

    def local_copy(index):
        return pltpu.make_async_copy(piece(index), slot(index, 0), local_sems.at[index])

    def shared_rows(full, owner):
        rows = full.shape[0] // shards
        return full.at[pl.ds(pl.multiple_of(owner * rows, rows), rows), :]

    shared = ((projection_piece, projection_full), (attended_piece, attended_full))
    other = lax.rem(shard + side, shards)

    def shared_copy(index, kind):
        held, full = shared[index]
        source = shared_rows(full, other) if kind == 2 else held
        target = shared_rows(full, other if kind == 2 else shard)
        return add_remote(
            source,
            target,
            shared_send.at[index, kind],
            shared_arrive.at[index, kind],
            across if kind == 0 else near,
        )

    def shared_local(index):
        held, full = shared[index]
        return pltpu.make_async_copy(held, shared_rows(full, shard), local_sems.at[len(chunks) + index])

    def grad_copy(step):
        return add_remote(
            sent_grads.at[step],
            grads_out.at[me],
            grad_send.at[step],
            grad_arrive.at[step],
            device_of(paired(me, step, members)),
        )

    own_grads = pltpu.make_async_copy(sent_grads.at[0], grads_out.at[me], grad_send.at[0])

    def start_distant(index):
        @pl.when(native_here)
        def _():
            distant_copy(index, slot(index, 0)).start()

        @pl.when(jnp.logical_not(native_here))
        def _():
            distant_copy(index, passing(index)).start()

    def pass_on(index):
        @pl.when(native_here)
        def _():
            distant_copy(index, passing(index)).wait_recv()
            across_copy(index, passing(index)).start()
            near_copy(index, 0, piece(index)).start()

        @pl.when(jnp.logical_not(native_here))
        def _():
            distant_copy(index, slot(index, 0)).wait_recv()
            near_copy(index, 0, slot(index, 0)).start()

    def finish(index):
        across_copy(index, passing(index)).wait_recv()
        near_copy(index, 1, slot(index, 1)).start()

    def held_rows(member):
        places = lax.broadcasted_iota(jnp.int32, (capacity, tokens), 0).astype(f32)
        return (counts[pl.ds(member, 1), :] == places).astype(bf16)

    barrier = pltpu.get_barrier_semaphore()
    for device in (across, near, distant):
        pl.semaphore_signal(barrier, inc=1, device_id=device, device_id_type=mesh_ids)

    @pl.loop(1, members)
    def _(step):
        device = device_of(paired(me, step, members))
        pl.semaphore_signal(barrier, inc=1, device_id=device, device_id_type=mesh_ids)

    for index in range(2):
        shared_local(index).start()

    @pl.when(native_here)
    def _():
        for index in chunks:
            local_copy(index).start()

    pl.semaphore_wait(barrier, members + 2)
    shared_copy(0, 0).start()
    shared_copy(0, 1).start()
    for index in range(3):
        start_distant(index)
    shared_copy(1, 0).start()
    shared_copy(1, 1).start()

    tile_rows = tile

    @pl.loop(0, tokens // tile_rows)
    def _(part):
        rows = pl.ds(pl.multiple_of(part * tile_rows, tile_rows), tile_rows)
        values = residual_ref[rows, :]
        scale = lax.rsqrt(jnp.mean(values * values, axis=1, keepdims=True) + epsilon)
        normed[rows, :] = (values * scale * gains_ref[:1, :]).astype(bf16)
        low_grads[rows, :] = out_grad_ref[rows, :].astype(bf16)

    names = lax.broadcasted_iota(jnp.int32, (members, tokens), 0)
    member = (route_rows[:1, :] == names) | (route_rows[1:, :] == names)
    earlier = lax.broadcasted_iota(jnp.int32, (tokens, tokens), 0) < lax.broadcasted_iota(
        jnp.int32, (tokens, tokens), 1
    )
    ranks = dot_nn(member.astype(bf16), earlier.astype(bf16))
    counts[...] = jnp.where(member, ranks, -1.0)

    @pl.loop(0, members)
    def _(step):
        block = dot_nn(held_rows(paired(me, step, members)), low_grads[...])
        sent_grads[step] = block.astype(bf16)

    shared_copy(0, 0).wait_recv()
    shared_copy(0, 2).start()
    own_grads.start()

    @pl.loop(1, members)
    def _(step):
        grad_copy(step).start()

    column = turned_row(row_ref[...])
    for start_row in range(0, tokens, tile):
        start = key_start(start_row)
        span_width = start_row + tile - start
        others = row_ref[:, start : start_row + tile].astype(f32)
        same = column[start_row : start_row + tile, :1] == others
        ahead = lax.broadcasted_iota(jnp.int32, (tile, span_width), 1) - (start_row - start)
        later = ahead > lax.broadcasted_iota(jnp.int32, (tile, span_width), 0)
        mask_ref[start_row : start_row + tile, :span_width] = jnp.where(
            same & jnp.logical_not(later), 0.0, masked
        )
    logs[...] = jnp.zeros_like(logs)
    shared_local(0).wait()
    shared_copy(0, 1).wait_recv()
    shared_copy(0, 2).wait_recv()

    @pl.loop(0, 3 * width // tile)
    def _(part):
        columns = pl.ds(pl.multiple_of(part * tile, tile), tile)
        projected[:, columns] = dot_nn(normed[...], projection_full[:, columns]).astype(bf16)

    @pl.when(jnp.logical_not(native_here))
    def _():
        for index in chunks:
            across_copy(index, piece(index)).start()

    shared_copy(1, 0).wait_recv()
    shared_copy(1, 2).start()
    outs = (
        (projection_full, projection_out),
        (attended_full, attended_out),
        (projected, projected_out),
        (merged, merged_out),
        (logs, logs_out),
        (hidden, hidden_out),
        (normed, normed_out),
        (normed2, normed2_out),
        (counts, counts_out),
        (sent, sent_out),
        (gate_rows, gates_out),
    )

    def keep(index):
        return pltpu.make_async_copy(*outs[index], out_sems.at[index])

    for index in (0, 2, 6, 8):
        keep(index).start()
    pairs = width // lanes

    def attend(first_pair, last_pair):
        @pl.loop(first_pair, last_pair)
        def _(pair):
            columns = [
                pl.ds(pl.multiple_of(group * width + pair * lanes, lanes), lanes)
                for group in range(3)
            ]
            attend_forward_pair(
                head_dim,
                pair,
                projected.at[:, columns[0]],
                projected.at[:, columns[1]],
                projected.at[:, columns[2]],
                base_ref.at[pair],
                merged.at[:, columns[0]],
                logs,
                mask_ref,
            )

    attend(0, pairs // 2)
    for index in range(2):
        pass_on(index)
        start_distant(index + 3)
    attend(pairs // 2, pairs)
    shared_local(1).wait()
    shared_copy(1, 1).wait_recv()
    shared_copy(1, 2).wait_recv()
    for index in (1, 3, 4):
        keep(index).start()

    @pl.loop(0, width // tile)
    def _(part):
        columns = pl.ds(pl.multiple_of(part * tile, tile), tile)
        hidden[:, columns] = residual_ref[:, columns] + dot_nn(
            merged[...], attended_full[:, columns]
        )

    for index in range(2, 4):
        pass_on(index)
        start_distant(index + 3)
    keep(5).start()

    @pl.loop(0, tokens // tile_rows)
    def _(part):
        rows = pl.ds(pl.multiple_of(part * tile_rows, tile_rows), tile_rows)
        values = hidden[rows, :]
        scale = lax.rsqrt(jnp.mean(values * values, axis=1, keepdims=True) + epsilon)
        normed2[rows, :] = (values * scale * gains_ref[1:, :]).astype(bf16)

    keep(7).start()

    logits = dot_nt(router_ref[...], normed2[...])[:members, :]
    first, second = route_rows[:1, :] == names, route_rows[1:, :] == names
    lean = jnp.sum(jnp.where(first, logits, 0.0), axis=0, keepdims=True)
    lean = lean - jnp.sum(jnp.where(second, logits, 0.0), axis=0, keepdims=True)
    gate_table[...] = jnp.where(first, jax.nn.sigmoid(lean), 0.0) + jnp.where(
        second, jax.nn.sigmoid(-lean), 0.0
    )
    gate_rows[...] = jnp.zeros_like(gate_rows)

    @pl.loop(0, members)
    def _(member_index):
        held = held_rows(member_index)
        sent[member_index] = dot_nn(held, normed2[...]).astype(bf16)
        digits = split_digits(gate_table[pl.ds(member_index, 1), :])
        sums = jnp.sum(dot_nt(digits, held), axis=0, keepdims=True)
        gate_rows[member_index, :1, :capacity] = sums

    keep(9).start()
    keep(10).start()
    for index in range(4):
        finish(index)
    for index in range(4, 8):
        pass_on(index)
        if index + 3 < len(chunks):
            start_distant(index + 3)
        if index > 4:
            finish(index - 1)
    finish(len(chunks) - 1)

    own_grads.wait()

    @pl.loop(1, members)
    def _(step):
        grad_copy(step).wait()

    for index in range(len(outs)):
        keep(index).wait()
    for index in range(2):
        for kind in range(3):
            shared_copy(index, kind).wait_send()
    for index in chunks:
        distant_copy(index, passing(index)).wait_send()
        across_copy(index, passing(index)).wait_send()
        for which in range(2):
            near_copy(index, which, slot(index, which)).wait()

    @pl.when(native_here)
    def _():
        for index in chunks:
            local_copy(index).wait()


def run_front(
    residual_in,
    gains,
    projection_piece,
    attended_piece,
    inner_piece,
    outer_piece,
    route_rows,
    out_grad,
    marks,
    base_rows,
    router_turned,
    capacity,
    members,
    shards,
):
    tokens, width = residual_in.shape
    wide = projection_piece.shape[1]
    heads = base_rows.shape[0]
    pairs = width // lanes
    units = outer_piece.shape[0]
    whole = pl.BlockSpec(memory_space=pltpu.VMEM)
    anywhere = pl.BlockSpec(memory_space=pl.ANY)
    shape = jax.ShapeDtypeStruct
    held = [
        ((shards * projection_piece.shape[0], wide), bf16),
        ((shards * attended_piece.shape[0], width), bf16),
        ((tokens, wide), bf16),
        ((tokens, width), bf16),
        ((tokens, lanes), f32),
        ((tokens, width), f32),
        ((tokens, width), bf16),
        ((tokens, width), bf16),
        ((members, tokens), f32),
        ((members, capacity, width), bf16),
        ((members, 8, -(-capacity // lanes) * lanes), f32),
    ]
    dma = pltpu.SemaphoreType.DMA
    return pl.pallas_call(
        functools.partial(front_kernel, shards, width // heads),
        in_specs=[whole] * 2 + [anywhere] * 4 + [whole] * 5,
        out_specs=[anywhere] * 14,
        out_shape=[shape(*entry) for entry in held]
        + [
            shape((members, capacity, width), bf16),
            shape((width, shards * units), bf16),
            shape((shards * units, width), bf16),
        ],
        scratch_shapes=[pltpu.VMEM(*entry) for entry in held]
        + [
            pltpu.VMEM((members, capacity, width), bf16),
            pltpu.VMEM((tokens, width), bf16),
            pltpu.VMEM((tokens, span), f32),
            pltpu.VMEM((members, tokens), f32),
            pltpu.VMEM((2, units, width), bf16),
            dma((len(held),)),
            dma((10,)),
            dma((2, 3)),
            dma((2, 3)),
            dma((members,)),
            dma((members,)),
            dma((8,)),
            dma((8,)),
            dma((8,)),
            dma((8,)),
            dma((8, 2)),
            dma((8, 2)),
        ],
        compiler_params=pltpu.CompilerParams(
            collective_id=2, has_side_effects=True, vmem_limit_bytes=60 * 2**20
        ),
        cost_estimate=pl.CostEstimate(
            flops=2 * tokens * width * (wide + width) + 4 * members * capacity * tokens * width,
            bytes_accessed=20 * tokens * width,
            transcendentals=heads * tokens * tokens // 2,
        ),
    )(
        residual_in,
        gains,
        projection_piece,
        attended_piece,
        inner_piece,
        outer_piece,
        route_rows,
        out_grad,
        marks[None, :],
        base_rows.reshape(pairs, heads // pairs, span),
        router_turned,
    )


def held_tile(counts, capacity):
    places = lax.broadcasted_iota(jnp.int32, (capacity, counts.shape[1]), 0).astype(f32)
    blocks = [
        (counts[member : member + 1, :] == places).astype(bf16)
        for member in range(counts.shape[0])
    ]
    return jnp.concatenate(blocks, axis=0)


def row_scale(values):
    return lax.rsqrt(jnp.mean(values * values, axis=1, keepdims=True) + epsilon)


def back_kernel(
    shards,
    members,
    head_dim,
    capacity,
    reduce_here,
    projected,
    logs,
    row_ref,
    route_rows,
    base_ref,
    normed,
    normed2,
    merged,
    projection_full,
    attended_full,
    router_ref,
    gains_ref,
    counts_ref,
    gates_back,
    back_ref,
    out_grad_ref,
    gated_ref,
    residual_ref,
    hidden_ref,
    inner_mine,
    inner_crossed,
    outer_mine,
    outer_given,
    inner_distant,
    residual_out,
    block_out,
    projection_out,
    attended_out,
    small_out,
    inner_final,
    outer_final,
    distant_in,
    outer_crossed,
    hidden_grad_ref,
    mask_ref,
    log_turned,
    dk_total,
    dv_total,
    diagonal,
    grads,
    merged_grad,
    attended_grad,
    attended_part,
    bias_rows,
    parts,
    first_in,
    second_in,
    results_tile,
    results_ref,
    near_in,
    far_in,
    halves,
    half_in,
    quads,
    quad_in,
    pieces,
    piece_in,
    finished,
    finished_in,
    quad_back,
    half_back,
    small_own,
    small_in,
    small_sum,
    stream_sems,
    distant_sems,
    across_sems,
    near_sems,
    far_sems,
    half_sems,
    back_sems,
    quad_sems,
    piece_sems,
    finished_sems,
    quad_back_sems,
    small_sems,
    result_send,
    result_arrive,
    back_load_sems,
    final_sems,
):
    tokens, width = normed.shape
    pairs = width // lanes
    group = width // shards
    expert, shard = lax.axis_index("expert"), lax.axis_index("shard")
    side, half = shards // 2, members // 2
    low, turn = lax.rem(shard, side), shard // side
    native_here = expert // half == turn
    across = {"shard": lax.rem(shard + side, shards)}
    near = {"shard": turn * side + lax.rem(low + 1, side)}
    distant = {"expert": lax.rem(expert + half, members)}
    odd, level = lax.rem(expert, 2), expert // 2
    beside = {"expert": expert + 1 - 2 * odd}
    low_level, top_level = lax.rem(level, 2), level // 2
    above = {"expert": (level + 1 - 2 * low_level) * 2 + odd}
    high, wide = group // 4, width // 2
    own_columns = pl.ds(pl.multiple_of(top_level * wide, lanes), wide)
    other_columns = pl.ds(pl.multiple_of((1 - top_level) * wide, lanes), wide)

    def distant_copy(matrix, source):
        top = width // 2 if matrix == 0 else 0
        return add_remote(
            source.at[top:, :],
            distant_in.at[matrix, top:, :],
            distant_sems.at[0, matrix],
            distant_sems.at[1, matrix],
            distant,
        )

    across_copy = add_remote(
        outer_given, outer_crossed, across_sems.at[0], across_sems.at[1], across
    )
    part_refs = [attended_part] + [parts.at[index] for index in range(3)]
    me, device_of = group_place(members, shards)

    def result_rows():
        start = pl.multiple_of(me * capacity, 16)
        return results_ref.at[pl.ds(start, capacity), :]

    def result_copy(step):
        member = paired(me, step, members)
        return add_remote(
            gated_ref.at[member],
            result_rows(),
            result_send.at[step],
            result_arrive.at[step],
            device_of(member),
        )

    own_result = pltpu.make_async_copy(gated_ref.at[me], result_rows(), result_send.at[0])
    count = len(part_refs)

    def near_copy(index, top):
        start = pl.multiple_of((2 * top + 1 - low) * group, group)
        return add_remote(
            part_refs[index].at[pl.ds(start, group), :],
            near_in.at[index, top],
            near_sems.at[0, index, top],
            near_sems.at[1, index, top],
            near,
        )

    def far_copy(index):
        return add_remote(
            near_in.at[index, 1 - turn],
            far_in.at[index],
            far_sems.at[0, index],
            far_sems.at[1, index],
            across,
        )

    def half_copy(index):
        return add_remote(
            halves.at[index, 1 - odd],
            half_in.at[index],
            half_sems.at[0, index],
            half_sems.at[1, index],
            beside,
        )

    def quad_copy(index):
        return add_remote(
            quads.at[index, 1 - low_level],
            quad_in.at[index],
            quad_sems.at[0, index],
            quad_sems.at[1, index],
            above,
        )

    def piece_copy(index):
        return add_remote(
            pieces.at[index, 1 - top_level],
            piece_in.at[index],
            piece_sems.at[0, index],
            piece_sems.at[1, index],
            distant,
        )

    def finished_copy(index):
        return add_remote(
            finished.at[index],
            finished_in.at[index],
            finished_sems.at[0, index],
            finished_sems.at[1, index],
            distant,
        )

    def quad_back_copy(index):
        return add_remote(
            quads.at[index, low_level],
            quad_back.at[index],
            quad_back_sems.at[0, index],
            quad_back_sems.at[1, index],
            above,
        )

    def back_copy(index):
        return add_remote(
            halves.at[index, odd],
            half_back.at[index],
            back_sems.at[0, index],
            back_sems.at[1, index],
            beside,
        )

    def small_copy(stage):
        return add_remote(
            small_own if stage == 0 else small_sum.at[stage - 1],
            small_in.at[stage],
            small_sems.at[0, stage],
            small_sems.at[1, stage],
            (near, across, beside, above, distant)[stage],
        )

    def start_near(index):
        if reduce_here:
            for top in range(2):
                near_copy(index, top).start()

    def near_to_far(index):
        if reduce_here:
            for top in range(2):
                near_copy(index, top).wait_recv()
                start = pl.multiple_of((2 * top + low) * group, group)
                own = part_refs[index][pl.ds(start, group), :].astype(f32)
                near_in[index, top] = (own + near_in[index, top].astype(f32)).astype(bf16)
            far_copy(index).start()

    def far_to_half(index):
        if reduce_here:
            far_copy(index).wait_recv()
            total = near_in[index, turn].astype(f32) + far_in[index].astype(f32)
            total = total.astype(bf16)
            for place in range(2):
                halves[index, place] = total[2 * place * high : 2 * (place + 1) * high, :]
            half_copy(index).start()

    def half_to_quad(index):
        if reduce_here:
            half_copy(index).wait_recv()
            total = halves[index, odd].astype(f32) + half_in[index].astype(f32)
            total = total.astype(bf16)
            for place in range(2):
                quads[index, place] = total[place * high : (place + 1) * high, :]
            quad_copy(index).start()

    def quad_to_piece(index):
        if reduce_here:
            quad_copy(index).wait_recv()
            total = quads[index, low_level].astype(f32) + quad_in[index].astype(f32)
            total = total.astype(bf16)
            for place in range(2):
                pieces[index, place] = total[:, place * wide : (place + 1) * wide]
            piece_copy(index).start()

    def piece_to_finished(index):
        if reduce_here:
            piece_copy(index).wait_recv()
            total = pieces[index, top_level].astype(f32) + piece_in[index].astype(f32)
            finished[index] = total.astype(bf16)
            finished_copy(index).start()

    def finished_to_quad(index):
        if reduce_here:
            finished_copy(index).wait_recv()
            quads[index, low_level, :, own_columns] = finished[index]
            quads[index, low_level, :, other_columns] = finished_in[index]
            quad_back_copy(index).start()

    def quad_to_back(index):
        if reduce_here:
            quad_back_copy(index).wait_recv()
            own = pl.ds(pl.multiple_of(low_level * high, 16), high)
            other = pl.ds(pl.multiple_of((1 - low_level) * high, 16), high)
            halves[index, odd, own, :] = quads[index, low_level]
            halves[index, odd, other, :] = quad_back[index]
            back_copy(index).start()

    def write_out(index):
        if reduce_here:
            back_copy(index).wait_recv()
            for place, block in ((odd, halves.at[index, odd]), (1 - odd, half_back.at[index])):
                rows = pl.ds(pl.multiple_of(place * 2 * high, 2 * high), 2 * high)
                values = block[...].astype(f32)
                if index == 0:
                    attended_out[rows, :] = values
                else:
                    projection_out[rows, (index - 1) * width : index * width] = values

    def small_step(stage):
        if reduce_here:
            small_copy(stage).wait_recv()
            own = small_own[...] if stage == 0 else small_sum[stage - 1]
            small_sum[stage] = own + small_in[stage]
            if stage < 4:
                small_copy(stage + 1).start()

    barrier = pltpu.get_barrier_semaphore()
    partners = [across, distant]
    if reduce_here:
        partners = [across, near, beside, above, distant]
    for device in partners:
        pl.semaphore_signal(barrier, inc=1, device_id=device, device_id_type=mesh_ids)

    @pl.loop(1, members)
    def _(step):
        device = device_of(paired(me, step, members))
        pl.semaphore_signal(barrier, inc=1, device_id=device, device_id_type=mesh_ids)

    own_result.start()
    pl.semaphore_wait(barrier, len(partners) + members - 1)

    across_copy.start()

    @pl.when(native_here)
    def _():
        distant_copy(0, inner_crossed).start()

    @pl.when(jnp.logical_not(native_here))
    def _():
        distant_copy(0, inner_mine).start()
        distant_copy(1, outer_mine).start()

    def load_rows(source, target, part, kind):
        return pltpu.make_async_copy(
            source.at[part * tile : (part + 1) * tile, :],
            target.at[part % 2],
            stream_sems.at[kind, part % 2],
        )

    def store_rows(target, part):
        return pltpu.make_async_copy(
            results_tile.at[part % 2],
            target.at[part * tile : (part + 1) * tile, :],
            stream_sems.at[2, part % 2],
        )

    row_parts = tokens // tile
    back_count = members * capacity
    back_loads = [
        pltpu.make_async_copy(
            back_ref.at[top : min(top + tokens, back_count), :],
            grads.at[top // tokens, : min(tokens, back_count - top), :],
            back_load_sems.at[top // tokens],
        )
        for top in range(0, back_count, tokens)
    ]
    for copy in back_loads:
        copy.start()
    for part in range(2):
        load_rows(hidden_ref, first_in, part, 0).start()
        load_rows(out_grad_ref, second_in, part, 1).start()

    log_turned[...] = logs[...].T
    column = turned_row(row_ref[...])
    for first in range(0, tokens, tile):
        start = key_start(first)
        span_width = first + tile - start
        own_marks = row_ref[:, first : first + tile].astype(f32)
        same = column[start : first + tile, :1] == own_marks
        ahead = lax.broadcasted_iota(jnp.int32, (span_width, tile), 0) - (first - start)
        later = ahead > lax.broadcasted_iota(jnp.int32, (span_width, tile), 1)
        mask_ref[:span_width, first : first + tile] = jnp.where(
            same & jnp.logical_not(later), 0.0, masked
        )
    small_own[...] = jnp.zeros_like(small_own)
    bias_top = small_own.shape[0] - pairs * bias_rows.shape[1]
    lane = lax.broadcasted_iota(jnp.int32, (tile, lanes), 1).astype(f32)
    for copy in back_loads:
        copy.wait()

    def middle_rows(part):
        rows = slice(part * tile, (part + 1) * tile)
        held = held_tile(counts_ref[:, rows], capacity)
        combined = functools.reduce(
            jnp.add,
            [
                dot_tn(
                    held[top : min(top + tokens, back_count), :],
                    grads[top // tokens, : min(tokens, back_count - top), :],
                )
                for top in range(0, back_count, tokens)
            ],
        )
        first, second = route_rows[:1, rows], route_rows[1:, rows]
        difference = jnp.zeros((1, tile), f32)
        for member in range(members):
            digits = split_digits(gates_back[member, :1, :capacity])
            sums = dot_nn(digits, held[member * capacity : (member + 1) * capacity, :])
            sums = jnp.sum(sums, axis=0, keepdims=True)
            difference = difference + jnp.where(jnp.minimum(first, second) == member, sums, -sums)
        difference = turned_row(difference)[:, :1]
        first, second = turned_row(first)[:, :1], turned_row(second)[:, :1]
        least, most = jnp.minimum(first, second), jnp.maximum(first, second)
        signs = (lane == least).astype(f32) - (lane == most).astype(f32)
        values = normed2[rows, :]
        lean = jnp.sum(dot_nt(values, router_ref[...]) * signs, axis=1, keepdims=True)
        gates = jax.nn.sigmoid(lean)
        logit_grad = gates * (1.0 - gates) * difference * signs
        above = logit_grad.astype(bf16)
        below = (logit_grad - above.astype(f32)).astype(bf16)
        router_grad = dot_tn(above, values) + dot_tn(below, values)
        small_own[2:bias_top, :] += router_grad[: bias_top - 2, :]
        gradient = dot_nn(above, router_ref[...]) + dot_nn(below, router_ref[...]) + combined
        load_rows(hidden_ref, first_in, part, 0).wait()
        load_rows(out_grad_ref, second_in, part, 1).wait()
        hidden = first_in[part % 2]
        scale = row_scale(hidden)
        weighted = gradient * gains_ref[1:, :]
        inner = jnp.mean(weighted * hidden, axis=1, keepdims=True)
        small_own[1:2, :] += jnp.sum(gradient * hidden * scale, axis=0, keepdims=True)
        if part >= 2:
            store_rows(hidden_grad_ref, part - 2).wait()
        hidden_grad = (
            second_in[part % 2] + scale * weighted - hidden * (scale * scale * scale * inner)
        )
        results_tile[part % 2] = hidden_grad
        store_rows(hidden_grad_ref, part).start()
        if part + 2 < row_parts:
            load_rows(hidden_ref, first_in, part + 2, 0).start()
            load_rows(out_grad_ref, second_in, part + 2, 1).start()
        low_grad = hidden_grad.astype(bf16)
        attended_grad[rows, :] = low_grad
        merged_grad[rows, :] = dot_nt(low_grad, attended_full[...]).astype(bf16)

    for part in range(row_parts):
        middle_rows(part)

    @pl.loop(0, width // tile)
    def _(part):
        columns = pl.ds(pl.multiple_of(part * tile, tile), tile)
        attended_part[:, columns] = dot_tn(merged[...], attended_grad[:, columns]).astype(bf16)

    start_near(0)
    for part in range(row_parts - 2, row_parts):
        store_rows(hidden_grad_ref, part).wait()

    def attend(first_pair, last_pair):
        @pl.loop(first_pair, last_pair)
        def _(pair):
            columns = [
                pl.ds(pl.multiple_of(place * width + pair * lanes, lanes), lanes)
                for place in range(3)
            ]
            own = columns[0]
            attend_backward_pair(
                head_dim,
                pair,
                projected.at[:, columns[0]],
                projected.at[:, columns[1]],
                projected.at[:, columns[2]],
                merged_grad.at[:, own],
                base_ref.at[pair],
                grads.at[0, :, own],
                grads.at[1, :, own],
                grads.at[2, :, own],
                bias_rows.at[pair],
                mask_ref,
                log_turned,
                dk_total,
                dv_total,
                diagonal,
            )

    @pl.loop(1, members)
    def _(step):
        result_copy(step).start()

    attend(0, pairs // 2)
    near_to_far(0)

    @pl.when(native_here)
    def _():
        across_copy.wait_recv()
        distant_copy(1, outer_crossed).start()

    attend(pairs // 2, pairs)
    far_to_half(0)
    for index in range(3):
        @pl.loop(0, width // tile)
        def _(part):
            columns = pl.ds(pl.multiple_of(part * tile, tile), tile)
            parts[index, :, columns] = dot_tn(normed[...], grads[index, :, columns]).astype(bf16)

        start_near(index + 1)
    per_pair = bias_rows.shape[1]
    for pair in range(pairs):
        top = bias_top + pair * per_pair
        small_own[top : top + per_pair, :] = bias_rows[pair]

    def norm_rows(part):
        rows = slice(part * tile, (part + 1) * tile)
        normed_grad = functools.reduce(
            jnp.add,
            [
                dot_nt(grads[index, rows, :], projection_full[:, index * width : (index + 1) * width])
                for index in range(3)
            ],
        )
        load_rows(residual_ref, first_in, part, 0).wait()
        load_rows(hidden_grad_ref, second_in, part, 1).wait()
        values = first_in[part % 2]
        scale = row_scale(values)
        weighted = normed_grad * gains_ref[:1, :]
        inner = jnp.mean(weighted * values, axis=1, keepdims=True)
        if part >= 2:
            store_rows(residual_out, part - 2).wait()
        results_tile[part % 2] = (
            second_in[part % 2] + scale * weighted - values * (scale * scale * scale * inner)
        )
        small_own[:1, :] += jnp.sum(normed_grad * values * scale, axis=0, keepdims=True)
        store_rows(residual_out, part).start()
        if part + 2 < tokens // tile:
            load_rows(residual_ref, first_in, part + 2, 0).start()
            load_rows(hidden_grad_ref, second_in, part + 2, 1).start()
        else:
            load_rows(hidden_ref, first_in, part % 2, 0).start()

    def block_rows(part):
        held = held_tile(counts_ref[:, part * tile : (part + 1) * tile], capacity)
        sums = dot_tn(held, results_ref[...])
        load_rows(hidden_ref, first_in, part, 0).wait()
        if part < 2:
            store_rows(residual_out, tokens // tile - 2 + part).wait()
        else:
            store_rows(block_out, part - 2).wait()
        results_tile[part % 2] = first_in[part % 2] + sums
        store_rows(block_out, part).start()
        if part + 2 < tokens // tile:
            load_rows(hidden_ref, first_in, part + 2, 0).start()

    def final_load(matrix, source, kind):
        target = (attended_grad, merged_grad)[kind]
        return pltpu.make_async_copy(source, target.at[:width, :], final_sems.at[matrix, kind])

    def start_final(matrix):
        mine, crossed = ((inner_mine, inner_crossed), (outer_mine, outer_crossed))[matrix]

        @pl.when(native_here)
        def _():
            final_load(matrix, mine, 0).start()

        @pl.when(jnp.logical_not(native_here))
        def _():
            if matrix == 1:
                across_copy.wait_recv()
            final_load(matrix, crossed, 0).start()

        distant_copy(matrix, inner_mine).wait_recv()
        for copy in distant_loads(matrix):
            copy.start()

    def distant_loads(matrix):
        middle = width // 2
        if matrix == 1:
            return [final_load(1, distant_in.at[1], 1)]
        return [
            pltpu.make_async_copy(
                inner_distant, merged_grad.at[:middle, :], final_sems.at[0, 1]
            ),
            pltpu.make_async_copy(
                distant_in.at[0, middle:, :],
                merged_grad.at[middle:width, :],
                final_sems.at[1, 3],
            ),
        ]

    final_stores = [
        pltpu.make_async_copy(
            diagonal.at[0], inner_final.at[: 2 * tile, :], final_sems.at[0, 2]
        ),
        pltpu.make_async_copy(
            diagonal.at[1, :tile, :], inner_final.at[2 * tile :, :], final_sems.at[0, 3]
        ),
        pltpu.make_async_copy(mask_ref.at[:, :width], outer_final, final_sems.at[1, 2]),
    ]

    def finish_final(matrix):
        for copy in [final_load(matrix, inner_mine, 0)] + distant_loads(matrix):
            copy.wait()
        for part in range(3):
            lines = slice(part * tile, (part + 1) * tile)
            sums = attended_grad[lines, :].astype(f32) + merged_grad[lines, :].astype(f32)
            if matrix == 1:
                mask_ref[:, lines] = sums.T
            else:
                diagonal[part // 2, part % 2 * tile : (part % 2 + 1) * tile, :] = sums
        for copy in final_stores[2:] if matrix == 1 else final_stores[:2]:
            copy.start()

    chunks = range(1, count)
    for part in range(2):
        load_rows(residual_ref, first_in, part, 0).start()
        load_rows(hidden_grad_ref, second_in, part, 1).start()
    half_to_quad(0)
    for index in chunks:
        near_to_far(index)
    for part in range(row_parts // 2):
        norm_rows(part)
    quad_to_piece(0)
    for index in chunks:
        far_to_half(index)
    for part in range(row_parts // 2, row_parts):
        norm_rows(part)
    if reduce_here:
        small_copy(0).start()
    piece_to_finished(0)
    for index in chunks:
        half_to_quad(index)
    own_result.wait()

    @pl.loop(1, members)
    def _(step):
        result_copy(step).wait()

    block_rows(0)
    small_step(0)
    for index in chunks:
        quad_to_piece(index)
    finished_to_quad(0)
    block_rows(1)
    small_step(1)
    for index in chunks:
        piece_to_finished(index)
    start_final(0)
    block_rows(2)
    small_step(2)
    quad_to_back(0)
    for index in chunks:
        finished_to_quad(index)
    for part in range(3, row_parts):
        block_rows(part)
    small_step(3)
    finish_final(0)
    for index in chunks:
        quad_to_back(index)
    small_step(4)
    start_final(1)
    finish_final(1)
    for index in range(count):
        write_out(index)
    if reduce_here:
        small_out[...] = small_sum[4]
    else:
        small_out[...] = small_own[...]
        for index in range(3):
            projection_out[:, index * width : (index + 1) * width] = parts[index]
        attended_out[...] = attended_part[...]

    for part in range(row_parts - 2, row_parts):
        store_rows(block_out, part).wait()
    across_copy.wait_send()
    for matrix in range(2):
        distant_copy(matrix, inner_mine).wait_send()
    for copy in final_stores:
        copy.wait()
    if reduce_here:
        for index in range(count):
            for top in range(2):
                near_copy(index, top).wait_send()
            far_copy(index).wait_send()
            back_copy(index).wait_send()
            half_copy(index).wait_send()
            quad_copy(index).wait_send()
            piece_copy(index).wait_send()
            finished_copy(index).wait_send()
            quad_back_copy(index).wait_send()
        for stage in range(5):
            small_copy(stage).wait_send()


def run_back(
    projected,
    logs,
    marks,
    route_rows,
    base_turned,
    normed,
    normed2,
    merged,
    projection_full,
    attended_full,
    router,
    gains,
    counts,
    gates_back,
    back,
    out_grad,
    gated,
    residual_in,
    hidden,
    weights,
    capacity,
    members,
    shards,
):
    tokens, width = normed.shape
    heads = base_turned.shape[0]
    pairs = width // lanes
    per_pair = heads // pairs
    group = width // shards
    units = weights[0].shape[1]
    small_shape = (-(-(2 + members + heads) // 8) * 8, width)
    reduce_here = members == 8 and shards == 4 and group % 64 == 0 and width % 256 == 0
    high, wide = group // 4, width // 2
    whole = pl.BlockSpec(memory_space=pltpu.VMEM)
    anywhere = pl.BlockSpec(memory_space=pl.ANY)
    shape = jax.ShapeDtypeStruct
    if reduce_here:
        sums = [shape((group, 3 * width), f32), shape((group, width), f32)]
    else:
        sums = [shape((width, 3 * width), bf16), shape((width, width), bf16)]
        high, wide = 16, lanes
    count = 4
    dma = pltpu.SemaphoreType.DMA
    vmem = pltpu.VMEM
    piece = (count, high, wide)
    quad = (count, high, 2 * wide)
    outs = pl.pallas_call(
        functools.partial(
            back_kernel, shards, members, width // heads, capacity, reduce_here
        ),
        in_specs=[whole] * 14 + [anywhere] * 10,
        out_specs=[anywhere] * 2 + [whole] * 3 + [anywhere] * 5,
        out_shape=[shape((tokens, width), f32)] * 2
        + sums
        + [
            shape(small_shape, f32),
            shape((width, units), f32),
            shape((units, width), f32),
            shape((2, width, units), bf16),
            shape((width, units), bf16),
            shape((tokens, width), f32),
        ],
        scratch_shapes=[
            vmem((span, tokens), f32),
            vmem((lanes, tokens), f32),
            vmem((tokens, lanes), f32),
            vmem((tokens, lanes), f32),
            vmem((per_pair, 2 * tile, span), f32),
            vmem((3, tokens, width), bf16),
            vmem((tokens, width), bf16),
            vmem((tokens, width), bf16),
            vmem((width, width), bf16),
            vmem((pairs, per_pair, span), f32),
            vmem((3, width, width), bf16),
            vmem((2, tile, width), f32),
            vmem((2, tile, width), f32),
            vmem((2, tile, width), f32),
            vmem((members * capacity, width), bf16),
            vmem((count, 2, group, width), bf16),
            vmem((count, group, width), bf16),
            vmem((count, 2, 2 * high, 2 * wide), bf16),
            vmem((count, 2 * high, 2 * wide), bf16),
            vmem((count, 2, high, 2 * wide), bf16),
            vmem(quad, bf16),
            vmem((count, 2, high, wide), bf16),
            vmem(piece, bf16),
            vmem(piece, bf16),
            vmem(piece, bf16),
            vmem(quad, bf16),
            vmem((count, 2 * high, 2 * wide), bf16),
            vmem(small_shape, f32),
            vmem((5,) + small_shape, f32),
            vmem((5,) + small_shape, f32),
            dma((3, 2)),
            dma((2, 2)),
            dma((2,)),
            dma((2, count, 2)),
            dma((2, count)),
            dma((2, count)),
            dma((2, count)),
            dma((2, count)),
            dma((2, count)),
            dma((2, count)),
            dma((2, count)),
            dma((2, 5)),
            dma((members,)),
            dma((members,)),
            dma((4,)),
            dma((2, 4)),
        ],
        compiler_params=pltpu.CompilerParams(
            collective_id=4, has_side_effects=True, vmem_limit_bytes=62 * 2**20
        ),
        cost_estimate=pl.CostEstimate(
            flops=16 * tokens * tokens * width,
            bytes_accessed=40 * tokens * width,
            transcendentals=heads * tokens * tokens // 2,
        ),
    )(
        projected,
        logs,
        marks[None, :],
        route_rows,
        base_turned.reshape(pairs, per_pair, span),
        normed,
        normed2,
        merged,
        projection_full,
        attended_full,
        router,
        gains,
        counts,
        gates_back,
        back,
        out_grad,
        gated,
        residual_in,
        hidden,
        *weights,
    )
    return outs[:-3], reduce_here


def sum_rows(part):
    return lax.all_gather(
        lax.psum_scatter(part.astype(bf16), ("shard", "expert"), scatter_dimension=0, tiled=True),
        "expert",
        axis=0,
        tiled=True,
    ).astype(f32)


def per_device(
    residual_in,
    norm1_gain,
    w_projection,
    rel_bias,
    w_attn_out,
    norm2_gain,
    w_router,
    expert_in,
    expert_out,
    segments,
    routes,
    out_grad,
):
    highest = lax.Precision.HIGHEST
    tokens_here, width = residual_in.shape
    heads, buckets = rel_bias.shape
    experts_all = w_router.shape[1]
    capacity = -(-5 * tokens_here // (32 * experts_all)) * 16
    marks = segments.reshape(-1)
    experts = jnp.arange(experts_all, dtype=jnp.int32)
    table_rows, table_turned = bias_tables(buckets)

    gains = jnp.stack([norm1_gain, norm2_gain])
    router = jnp.pad(w_router.T, ((0, -experts_all % lanes), (0, 0)))
    route_rows = routes.T
    base_rows = jnp.dot(rel_bias, table_rows.T, precision=highest)
    base_turned = jnp.dot(rel_bias, table_turned.T, precision=highest)
    (
        full_projection,
        full_attn_out,
        projected,
        merged,
        logs,
        hidden,
        normed,
        normed2,
        counts,
        sent,
        gate_rows,
        arrived_grad,
        inner,
        outer,
    ) = run_front(
        residual_in,
        gains,
        w_projection,
        w_attn_out,
        expert_in[0],
        expert_out[0],
        route_rows,
        out_grad,
        marks,
        base_rows,
        router,
        capacity,
        experts_all,
        lax.axis_size("shard"),
    )
    shards = lax.axis_size("shard")
    gated, back_rows, gates_back, *weights = run_experts(
        sent, gate_rows, arrived_grad, inner, outer, shards
    )
    inner_mine, outer_mine, outer_given, inner_crossed, inner_distant = weights
    filled = 2 + experts_all
    outs, reduced = run_back(
        projected,
        logs,
        marks,
        route_rows,
        base_turned,
        normed,
        normed2,
        merged,
        full_projection,
        full_attn_out,
        router,
        gains,
        counts,
        gates_back,
        back_rows.reshape(-1, width),
        out_grad,
        gated,
        residual_in,
        hidden,
        (inner_mine, inner_crossed, outer_mine, outer_given, inner_distant),
        capacity,
        experts_all,
        shards,
    )
    residual_grad, block_out, projection_total, attn_out_total, small = outs[:5]
    expert_in_grad, expert_out_grad = outs[5:]
    if not reduced:
        projection_total = sum_rows(projection_total)
        attn_out_total = sum_rows(attn_out_total)
        small = lax.psum(small, ("expert", "shard"))
    gain1_total, gain2_total = small[0], small[1]
    router_total = small[2:filled].T
    bias_total = jnp.dot(small[small.shape[0] - heads :], table_turned, precision=highest)
    return (
        block_out,
        residual_grad,
        gain1_total,
        projection_total,
        bias_total,
        attn_out_total,
        gain2_total,
        router_total,
        expert_in_grad[None],
        expert_out_grad[None],
    )


def solution(mesh):
    return jax.shard_map(
        per_device,
        mesh=mesh,
        in_specs=(
            P(("expert", "shard"), None),
            P(),
            P("shard", None),
            P(),
            P("shard", None),
            P(),
            P(),
            P("expert", None, "shard"),
            P("expert", "shard", None),
            P(("expert", "shard"), None),
            P(("expert", "shard"), None),
            P(("expert", "shard"), None),
        ),
        out_specs=(
            P(("expert", "shard"), None),
            P(("expert", "shard"), None),
            P(),
            P("shard", None),
            P(),
            P("shard", None),
            P(),
            P(),
            P("expert", None, "shard"),
            P("expert", "shard", None),
        ),
        check_vma=False,
    )
```

```python
import functools

import jax
import jax.numpy as jnp
import numpy as np
from jax import lax
from jax.experimental import pallas as pl
from jax.experimental.pallas import tpu as pltpu
from jax.sharding import PartitionSpec as P

bucket_borders = (19, 21, 24, 27, 31, 35, 40, 46, 52, 59, 67, 77, 87, 99, 113)
longest = 512
tile = 256
span = 3 * tile
lanes = 128
masked = -1e30
f32 = jnp.float32
bf16 = jnp.bfloat16


def one_hot_buckets(distance, buckets):
    distance = np.clip(distance, 0, None)
    beyond = sum((distance >= border).astype(np.int32) for border in bucket_borders)
    bucket = np.where(distance < 16, distance, 16 + beyond)
    return (bucket[:, None] == np.arange(buckets)[None, :]).astype(np.float32)


def bias_tables(buckets):
    lane = np.arange(span)
    rows = np.where(lane < 2 * tile, tile - lane, tile + span - lane)
    turned = np.where(lane < tile, tile + lane, tile + lane - span)
    return (one_hot_buckets(rows, buckets), one_hot_buckets(turned, buckets))


def key_start(first):
    return max(0, first - longest) // tile * tile


def dot_nt(a, b):
    return lax.dot_general(a, b, (((1,), (1,)), ((), ())), preferred_element_type=f32)


def dot_tn(a, b):
    return lax.dot_general(a, b, (((0,), (0,)), ((), ())), preferred_element_type=f32)


def dot_nn(a, b):
    return lax.dot_general(a, b, (((1,), (0,)), ((), ())), preferred_element_type=f32)


def attend_forward_pair(
    head_dim, pair, q_ref, k_ref, v_ref, base_ref, out_ref, log_ref, mask_ref
):
    seq_len = q_ref.shape[0]
    scale = head_dim ** (-0.5)
    per_pair = lanes // head_dim
    lane = lax.broadcasted_iota(jnp.int32, (tile, lanes), 1)
    tables = []
    for head in range(per_pair):
        wide = jnp.broadcast_to(base_ref[head : head + 1, :], (tile, span))
        tables.append(pltpu.roll(wide, 0, 1, stride=1, stride_axis=0))
    for first in range(0, seq_len, tile):
        start = key_start(first)
        merged = jnp.zeros((tile, lanes), f32)
        logs = log_ref[first : first + tile, :]
        for head in range(per_pair):
            inside = (lane >= head * head_dim) & (lane < (head + 1) * head_dim)
            query = jnp.where(inside, q_ref[first : first + tile, :] * scale, 0.0).astype(bf16)
            pieces = []
            for begin in range(start, first + tile, tile):
                piece = dot_nt(query, k_ref[begin : begin + tile, :])
                back = (first - begin) // tile
                if back == 0:
                    piece = piece + tables[head][:, tile : 2 * tile]
                elif back == 1:
                    piece = piece + tables[head][:, :tile]
                else:
                    piece = piece + base_ref[head : head + 1, :1]
                place = begin - start
                pieces.append(piece + mask_ref[first : first + tile, place : place + tile])
            peak = functools.reduce(jnp.maximum, pieces)
            peak = jnp.max(peak, axis=1, keepdims=True)
            weights = [jnp.exp(piece - peak) for piece in pieces]
            total = jnp.sum(functools.reduce(jnp.add, weights), axis=1, keepdims=True)
            mixed = jnp.zeros((tile, lanes), f32)
            for index, weight in enumerate(weights):
                begin = start + index * tile
                mixed = mixed + dot_nn(weight.astype(bf16), v_ref[begin : begin + tile, :])
            merged = jnp.where(inside, mixed * (1.0 / total), merged)
            logs = jnp.where(lane == pair * per_pair + head, peak + jnp.log(total), logs)
        out_ref[first : first + tile, :] = merged.astype(bf16)
        log_ref[first : first + tile, :] = logs


def attend_backward_pair(
    head_dim,
    pair,
    q_ref,
    k_ref,
    v_ref,
    grad_ref,
    base_ref,
    dq_ref,
    dk_ref,
    dv_ref,
    bias_ref,
    mask_ref,
    log_turned,
    dk_total,
    dv_total,
    diagonal,
):
    seq_len = q_ref.shape[0]
    scale = head_dim ** (-0.5)
    per_pair = lanes // head_dim
    firsts = range(0, seq_len, tile)
    dk_total[...] = jnp.zeros_like(dk_total)
    dv_total[...] = jnp.zeros_like(dv_total)
    lane = lax.broadcasted_iota(jnp.int32, (tile, lanes), 1)
    tables = []
    for head in range(per_pair):
        wide = jnp.broadcast_to(base_ref[head : head + 1, :], (2 * tile, span))
        tables.append(pltpu.roll(wide, 0, 1, stride=1, stride_axis=0)[:, :tile])
    diagonal[...] = jnp.zeros_like(diagonal)
    far = [jnp.zeros((1, tile), f32) for _ in range(per_pair)]
    for first in firsts:
        start = key_start(first)
        query_grad = jnp.zeros((tile, lanes), f32)
        for head in range(per_pair):
            inside = (lane >= head * head_dim) & (lane < (head + 1) * head_dim)

            def own(values):
                return jnp.where(inside, values, 0.0).astype(bf16)

            query = own(q_ref[first : first + tile, :] * scale)
            grad = own(grad_ref[first : first + tile, :])
            row = log_turned[pl.ds(pair * per_pair + head, 1), first : first + tile]
            begins = range(start, first + tile, tile)
            shares, dots = [], []
            inner = jnp.zeros((1, tile), f32)
            for begin in begins:
                piece = dot_nt(k_ref[begin : begin + tile, :], query)
                back = (first - begin) // tile
                if back == 0:
                    piece = piece + tables[head][tile:, :]
                elif back == 1:
                    piece = piece + tables[head][:tile, :]
                else:
                    piece = piece + base_ref[head : head + 1, :1]
                place = begin - start
                piece = piece + mask_ref[place : place + tile, first : first + tile]
                share = jnp.exp(piece - row)
                dot = dot_nt(v_ref[begin : begin + tile, :], grad)
                inner = inner + jnp.sum(share * dot, axis=0, keepdims=True)
                dv_total[begin : begin + tile, :] += dot_nn(share.astype(bf16), grad)
                shares.append(share)
                dots.append(dot)
            for begin, share, dot in zip(begins, shares, dots):
                back = (first - begin) // tile
                score_grad = share * (dot - inner)
                if back < 2:
                    top = (1 - back) * tile
                    diagonal[head, top : top + tile, :tile] += score_grad
                else:
                    far[head] = far[head] + jnp.sum(score_grad, axis=0, keepdims=True)
                score_grad = score_grad.astype(bf16)
                dk_total[begin : begin + tile, :] += dot_nn(score_grad, query)
                query_grad = query_grad + dot_tn(
                    score_grad, own(k_ref[begin : begin + tile, :] * scale)
                )
        dq_ref[first : first + tile, :] = query_grad.astype(bf16)
    dk_ref[...] = dk_total[...].astype(bf16)
    dv_ref[...] = dv_total[...].astype(bf16)
    for head in range(per_pair):
        grouped = diagonal[head, :8, :]
        for top in range(8, 2 * tile, 8):
            grouped = grouped + pltpu.roll(diagonal[head, top : top + 8, :], span - top, 1)
        sums = grouped[:1, :]
        for row in range(1, 8):
            sums = sums + pltpu.roll(grouped[row : row + 1, :], span - row, 1)
        bias_ref[head : head + 1, :tile] = sums[:, :tile] + far[head]
        bias_ref[head : head + 1, tile:] = sums[:, tile:]


hidden_tile = 768
block_count = 4
epsilon = 1e-06
mesh_ids = pl.DeviceIdType.MESH


def gelu_parts(values):
    factor = 0.7978845608028654
    squares = values * values
    turned = jnp.tanh(values * (factor + (factor * 0.044715) * squares))
    share = 0.5 + 0.5 * turned
    active = values * share
    inside = 2.0 * factor + (6.0 * factor * 0.044715) * squares
    return (active, share + active * ((1.0 - share) * inside))


def turned_row(row):
    return jnp.broadcast_to(row.astype(f32), (lanes, row.shape[1])).T


def split_digits(row):
    places = lax.broadcasted_iota(jnp.int32, (8, row.shape[1]), 0)
    digits = jnp.zeros(places.shape, f32)
    for place in range(3):
        digit = row.astype(bf16).astype(f32)
        digits = jnp.where(places == place, digit, digits)
        row = row - digit
    return digits.astype(bf16)


def paired(place, step, members):
    partner, bit = 0, 1
    while bit < members:
        ours, theirs = place // bit % 2, step // bit % 2
        partner = partner + bit * (ours + theirs - 2 * ours * theirs)
        bit = 2 * bit
    return partner


def group_place(members, shards):
    expert, shard = lax.axis_index("expert"), lax.axis_index("shard")
    half, side = members // 2, shards // 2

    def device_of(member):
        return {
            "expert": expert // half * half + lax.rem(member, half),
            "shard": member // half * side + lax.rem(shard, side),
        }

    return shard // side * half + lax.rem(expert, half), device_of


def add_remote(source, target, send, arrive, device):
    return pltpu.make_async_remote_copy(
        src_ref=source,
        dst_ref=target,
        send_sem=send,
        recv_sem=arrive,
        device_id=device,
        device_id_type=mesh_ids,
    )


def expert_kernel(
    shards,
    sent_ref,
    gates_ref,
    grads_ref,
    inner_ref,
    outer_ref,
    gated_out,
    back_out,
    gates_out,
    active_out,
    pre_out,
    inner_mine,
    outer_mine,
    outer_given,
    inner_crossed,
    inner_distant,
    rows,
    grads_held,
    scaled,
    actives,
    pres,
    gates_in,
    gates_back,
    value_total,
    row_total,
    inner_held,
    outer_held,
    turned,
    near_in,
    send_sems,
    arrive_sems,
    back_sems,
    returned_sems,
    gate_send,
    gate_arrive,
    digit_sems,
    digit_arrive,
    load_sems,
    weight_sems,
    active_sems,
    pre_sems,
    tile_sems,
    keep_sems,
    near_send,
    near_arrive,
    across_sems,
    distant_sems,
):
    members, capacity, _ = sent_ref.shape
    blocks, block, width = rows.shape
    units = actives.shape[2]
    quarters = actives.shape[1] // block
    block_steps = members // blocks
    me, device_of = group_place(members, shards)
    shard = lax.axis_index("shard")
    side = shards // 2
    low, turn = lax.rem(shard, side), shard // side
    far_low = lax.rem(low + 1, side)
    across = {"shard": lax.rem(shard + side, shards)}
    near = {"shard": turn * side + far_low}
    expert, half = lax.axis_index("expert"), members // 2
    native_here = expert // half == turn
    distant = {"expert": lax.rem(expert + half, members)}

    def source(step):
        return paired(me, step, members)

    def device(step):
        return device_of(source(step))

    def place_of(ref, step):
        start = pl.multiple_of(lax.rem(step, block_steps) * capacity, 16)
        return ref.at[step // block_steps, pl.ds(start, capacity)]

    def sending(step):
        return add_remote(
            sent_ref.at[source(step)],
            place_of(rows, step),
            send_sems.at[step],
            arrive_sems.at[step],
            device(step),
        )

    def sending_gates(step):
        return add_remote(
            gates_ref.at[source(step)],
            gates_in.at[step],
            gate_send.at[step],
            gate_arrive.at[step],
            device(step),
        )

    def returning(step):
        return add_remote(
            place_of(rows, step),
            back_out.at[me],
            back_sems.at[step],
            returned_sems.at[step],
            device(step),
        )

    def returning_gates(step):
        return add_remote(
            gates_back.at[step],
            gates_out.at[me],
            digit_sems.at[step],
            digit_arrive.at[step],
            device(step),
        )

    def loading(step):
        return pltpu.make_async_copy(
            grads_ref.at[source(step)], place_of(grads_held, step), load_sems.at[step]
        )

    def giving(step):
        return pltpu.make_async_copy(
            place_of(grads_held, step), gated_out.at[source(step)], load_sems.at[step]
        )

    def keeping(index, slot):
        return (
            pltpu.make_async_copy(actives.at[slot], active_out.at[index], active_sems.at[slot]),
            pltpu.make_async_copy(pres.at[slot], pre_out.at[index], pre_sems.at[slot]),
        )

    own_rows = pltpu.make_async_copy(sent_ref.at[me], place_of(rows, 0), arrive_sems.at[0])
    own_back = pltpu.make_async_copy(place_of(rows, 0), back_out.at[me], back_sems.at[0])
    own_digits = pltpu.make_async_copy(gates_back.at[0], gates_out.at[me], digit_sems.at[0])
    own_gates = pltpu.make_async_copy(gates_ref.at[me], gates_in.at[0], gate_arrive.at[0])
    weight_loads = (
        pltpu.make_async_copy(inner_ref, inner_held, weight_sems.at[0]),
        pltpu.make_async_copy(outer_ref, outer_held, weight_sems.at[1]),
    )
    barrier = pltpu.get_barrier_semaphore()
    for partner in (near, distant):
        pl.semaphore_signal(barrier, inc=1, device_id=partner, device_id_type=mesh_ids)

    @pl.loop(1, members)
    def _(step):
        pl.semaphore_signal(barrier, inc=1, device_id=device(step), device_id_type=mesh_ids)

    own_rows.start()
    own_gates.start()
    for copy in weight_loads:
        copy.start()

    @pl.loop(0, members)
    def _(step):
        loading(step).start()

    pl.semaphore_wait(barrier, members + 1)

    neighbours = [step for step in range(1, members) if step & (step - 1) == 0]
    for step in neighbours:
        sending_gates(step).start()
        sending(step).start()
    for copy in weight_loads:
        copy.wait()
    own_rows.wait()
    own_gates.wait()
    sending_gates(1).wait_recv()
    sending(1).wait_recv()
    for step in range(1, members):
        if step not in neighbours:
            sending_gates(step).start()
            sending(step).start()

    @pl.loop(0, blocks)
    def _(index):
        slot = lax.rem(index, 2)

        @pl.loop(0, block_steps)
        def _(place):
            step = index * block_steps + place

            @pl.when(step > 1)
            def _():
                sending_gates(step).wait_recv()
                sending(step).wait_recv()

            loading(step).wait()

        @pl.when(index > 1)
        def _():
            for copy in keeping(index - 2, slot):
                copy.wait()

        gates = jnp.concatenate(
            [
                turned_row(gates_in[index * block_steps + place, :1, :])[:capacity, :1]
                for place in range(block_steps)
            ],
            axis=0,
        )
        scaled[...] = (gates * grads_held[index].astype(f32)).astype(bf16)
        held_columns = pl.ds(pl.multiple_of(index * block, lanes), block)
        turned[0, :, held_columns] = rows[index].T
        turned[1, :, held_columns] = scaled[...].T
        value_total[...] = jnp.zeros_like(value_total)
        row_total[...] = jnp.zeros_like(row_total)

        def units_of(part):
            return pl.ds(pl.multiple_of(part * units, units), units)

        def block_of(part):
            return pl.ds(pl.multiple_of(part * block, 16), block)

        def begin_part(part):
            active, slope = gelu_parts(dot_nn(rows[index], inner_held[:, units_of(part)]))
            actives[slot, block_of(part), :] = active.astype(bf16)
            pre = dot_nt(scaled[...], outer_held[units_of(part), :]) * slope
            pres[slot, block_of(part), :] = pre.astype(bf16)

        def end_part(part):
            value_total[...] += dot_nn(actives[slot, block_of(part), :], outer_held[units_of(part), :])
            row_total[...] += dot_nt(pres[slot, block_of(part), :], inner_held[:, units_of(part)])

        begin_part(0)

        @pl.loop(1, quarters)
        def _(part):
            end_part(part - 1)
            begin_part(part)

        end_part(quarters - 1)
        for copy in keeping(index, slot):
            copy.start()
        produced = value_total[...]
        rows[index] = row_total[...].astype(bf16)
        rest = jnp.sum(grads_held[index].astype(f32) * produced, axis=1, keepdims=True)
        grads_held[index] = (gates * produced).astype(bf16)
        spare = gates_back.shape[2] - capacity
        for place in range(block_steps):
            wide = jnp.broadcast_to(
                rest[place * capacity : (place + 1) * capacity, :], (capacity, lanes)
            )
            wide = jnp.concatenate([wide, jnp.zeros((spare, lanes), f32)], axis=0)
            gates_back[index * block_steps + place] = wide.T[:8, :]

        @pl.loop(0, block_steps)
        def _(place):
            step = index * block_steps + place
            giving(step).start()

            @pl.when(step > 0)
            def _():
                returning(step).start()
                returning_gates(step).start()

            @pl.when(step == 0)
            def _():
                own_back.start()
                own_digits.start()

    held_parts = (inner_held, outer_held)
    targets = {(0, 3): inner_mine, (1, 3): outer_mine, (1, 2): outer_given}
    places = (2 * far_low, 2 * far_low + 1, 2 * low + 1, 2 * low)
    order = [(matrix, position) for matrix in range(2) for position in range(4)]
    buffers = (actives.at[0], pres.at[0], actives.at[1], pres.at[1])

    def part_of(matrix, position):
        if matrix == 0:
            return inner_held.at[:, position * units : (position + 1) * units]
        return outer_held.at[position * width : (position + 1) * width, :]

    def tile_loads(count):
        matrix, position = order[count]
        kept = (pre_out, active_out)[matrix]
        start = pl.multiple_of(places[position] * block, 16)
        return [
            pltpu.make_async_copy(
                kept.at[index, pl.ds(start, block), :],
                buffers[count % 4].at[index * block : (index + 1) * block, :],
                tile_sems.at[count % 4, index],
            )
            for index in range(blocks)
        ]

    def near_copy(matrix, position):
        return add_remote(
            part_of(matrix, position),
            near_in.at[matrix, position],
            near_send.at[matrix, position],
            near_arrive.at[matrix, position],
            near,
        )

    lines_each = width // 4

    def lines_of(index):
        return slice(index * lines_each, (index + 1) * lines_each)

    def across_copy(index):
        return add_remote(
            part_of(0, 2).at[lines_of(index), :],
            inner_crossed.at[lines_of(index), :],
            across_sems.at[0, index],
            across_sems.at[1, index],
            across,
        )

    def distant_copy(index, source):
        return add_remote(
            source.at[lines_of(index), :],
            inner_distant.at[lines_of(index), :],
            distant_sems.at[0, index],
            distant_sems.at[1, index],
            distant,
        )

    def pass_on(index):
        @pl.when(native_here)
        def _():
            across_copy(index).wait_recv()
            distant_copy(index, inner_crossed).start()

    def keep_copy(matrix, position):
        index = {(0, 3): 0, (1, 3): 1, (1, 2): 2}[matrix, position]
        return pltpu.make_async_copy(
            part_of(matrix, position), targets[matrix, position], keep_sems.at[index]
        )

    for index in range(blocks - 2, blocks):
        for copy in keeping(index, index % 2):
            copy.wait()
    for count in range(4):
        for copy in tile_loads(count):
            copy.start()
    for count, (matrix, position) in enumerate(order):
        for copy in tile_loads(count):
            copy.wait()
        target = part_of(matrix, position)

        @pl.loop(0, units // tile)
        def _(part):
            columns = pl.ds(pl.multiple_of(part * tile, tile), tile)
            sums = dot_nn(turned[matrix], buffers[count % 4][:, columns])
            target[:, columns] = sums.astype(bf16)

        if count + 4 < len(order):
            for copy in tile_loads(count + 4):
                copy.start()
        if position < 2:
            near_copy(matrix, position).start()
        else:
            other = 3 - position
            near_copy(matrix, other).wait_recv()

            @pl.loop(0, width // tile)
            def _(part):
                lines = pl.ds(pl.multiple_of(part * tile, tile), tile)
                sums = target[lines, :].astype(f32) + near_in[matrix, other, lines, :].astype(f32)
                target[lines, :] = sums.astype(bf16)

            if (matrix, position) == (0, 2):
                for index in range(4):
                    across_copy(index).start()
            else:
                keep_copy(matrix, position).start()
            if (matrix, position) == (0, 3):

                @pl.when(jnp.logical_not(native_here))
                def _():
                    for index in range(2):
                        distant_copy(index, part_of(0, 3)).start()

        if count in (4, 6):
            pass_on((count - 4) // 2)

    own_back.wait()
    own_digits.wait()

    @pl.loop(1, members)
    def _(step):
        sending_gates(step).wait_send()
        sending(step).wait_send()
        returning(step).wait()
        returning_gates(step).wait()

    @pl.loop(0, members)
    def _(step):
        giving(step).wait()

    for matrix, position in targets:
        keep_copy(matrix, position).wait()
    @pl.when(jnp.logical_not(native_here))
    def _():
        for index in range(2):
            across_copy(index).wait_recv()

    for index in range(4):
        across_copy(index).wait_send()
        if index < 2:
            distant_copy(index, inner_crossed).wait()
        else:
            across_copy(index).wait_recv()
    for matrix in range(2):
        for position in range(2):
            near_copy(matrix, position).wait_send()


def run_experts(sent, gates, grads, inner, outer, shards):
    members, capacity, width = sent.shape
    hidden_units = inner.shape[1]
    units = hidden_units // shards
    blocks = block_count
    block = members // blocks * capacity
    anywhere = pl.BlockSpec(memory_space=pl.ANY)
    shape = jax.ShapeDtypeStruct
    hidden_shape = shape((blocks, shards * block, units), bf16)
    piece = shape((width, units), bf16)
    dma = pltpu.SemaphoreType.DMA
    outs = pl.pallas_call(
        functools.partial(expert_kernel, shards),
        in_specs=[anywhere] * 5,
        out_specs=[anywhere] * 10,
        out_shape=[
            shape((members, capacity, width), bf16),
            shape((members, capacity, width), bf16),
            shape(gates.shape, f32),
            hidden_shape,
            hidden_shape,
            piece,
            piece,
            piece,
            piece,
            shape((width // 2, units), bf16),
        ],
        scratch_shapes=[
            pltpu.VMEM((blocks, block, width), bf16),
            pltpu.VMEM((blocks, block, width), bf16),
            pltpu.VMEM((block, width), bf16),
            pltpu.VMEM((2, shards * block, units), bf16),
            pltpu.VMEM((2, shards * block, units), bf16),
            pltpu.VMEM(gates.shape, f32),
            pltpu.VMEM(gates.shape, f32),
            pltpu.VMEM((block, width), f32),
            pltpu.VMEM((block, width), f32),
            pltpu.VMEM((width, hidden_units), bf16),
            pltpu.VMEM((hidden_units, width), bf16),
            pltpu.VMEM((2, width, blocks * block), bf16),
            pltpu.VMEM((2, 2, width, units), bf16),
            dma((members,)),
            dma((members,)),
            dma((members,)),
            dma((members,)),
            dma((members,)),
            dma((members,)),
            dma((members,)),
            dma((members,)),
            dma((members,)),
            dma((2,)),
            dma((2,)),
            dma((2,)),
            dma((4, blocks)),
            dma((3,)),
            dma((2, 2)),
            dma((2, 2)),
            dma((2, 4)),
            dma((2, 2)),
        ],
        compiler_params=pltpu.CompilerParams(
            collective_id=0, has_side_effects=True, vmem_limit_bytes=63 * 2**20
        ),
        cost_estimate=pl.CostEstimate(
            flops=12 * members * capacity * width * hidden_units,
            bytes_accessed=2 * (members * capacity * (6 * width + 4 * hidden_units)),
            transcendentals=members * capacity * hidden_units,
        ),
    )(sent, gates, grads, inner, outer)
    return outs[:3] + outs[5:]


def front_kernel(
    shards,
    head_dim,
    residual_ref,
    gains_ref,
    projection_piece,
    attended_piece,
    inner_piece,
    outer_piece,
    route_rows,
    out_grad_ref,
    row_ref,
    base_ref,
    router_ref,
    projection_out,
    attended_out,
    projected_out,
    merged_out,
    logs_out,
    hidden_out,
    normed_out,
    normed2_out,
    counts_out,
    sent_out,
    gates_out,
    grads_out,
    inner_out,
    outer_out,
    projection_full,
    attended_full,
    projected,
    merged,
    logs,
    hidden,
    normed,
    normed2,
    counts,
    sent,
    gate_rows,
    sent_grads,
    low_grads,
    mask_ref,
    gate_table,
    given,
    out_sems,
    local_sems,
    shared_send,
    shared_arrive,
    grad_send,
    grad_arrive,
    distant_send,
    distant_arrive,
    across_send,
    across_arrive,
    near_send,
    near_arrive,
):
    tokens, width = residual_ref.shape
    members, capacity, _ = grads_out.shape
    expert, shard = lax.axis_index("expert"), lax.axis_index("shard")
    side, half = shards // 2, members // 2
    me, device_of = group_place(members, shards)
    low, turn = lax.rem(shard, side), shard // side
    native_here = expert // half == turn
    across = {"shard": lax.rem(shard + side, shards)}
    near = {"shard": turn * side + lax.rem(low + 1, side)}
    distant = {"expert": lax.rem(expert + half, members)}
    pieces = (inner_piece, outer_piece)
    units = outer_piece.shape[0]
    per_piece = 4
    chunk_rows = width // per_piece
    chunks = range(2 * per_piece)

    def piece(index):
        start = index % per_piece * chunk_rows
        return pieces[index // per_piece].at[start : start + chunk_rows, :]

    def slot(index, which):
        place = 2 * low + which
        start = index % per_piece * chunk_rows
        if index // per_piece == 0:
            columns = pl.ds(pl.multiple_of(place * units, units), units)
            return inner_out.at[start : start + chunk_rows, columns]
        return outer_out.at[pl.ds(pl.multiple_of(place * units + start, chunk_rows), chunk_rows), :]

    def passing(index):
        start = index % per_piece * chunk_rows
        return given.at[index // per_piece, start : start + chunk_rows, :]

    def distant_copy(index, target):
        return add_remote(
            piece(index), target, distant_send.at[index], distant_arrive.at[index], distant
        )

    def across_copy(index, source):
        return add_remote(
            source, slot(index, 1), across_send.at[index], across_arrive.at[index], across
        )

    def near_copy(index, which, source):
        return add_remote(
            source,
            slot(index, which),
            near_send.at[index, which],
            near_arrive.at[index, which],
            near,
        )

    def local_copy(index):
        return pltpu.make_async_copy(piece(index), slot(index, 0), local_sems.at[index])

    def shared_rows(full, owner):
        rows = full.shape[0] // shards
        return full.at[pl.ds(pl.multiple_of(owner * rows, rows), rows), :]

    shared = ((projection_piece, projection_full), (attended_piece, attended_full))
    other = lax.rem(shard + side, shards)

    def shared_copy(index, kind):
        held, full = shared[index]
        source = shared_rows(full, other) if kind == 2 else held
        target = shared_rows(full, other if kind == 2 else shard)
        return add_remote(
            source,
            target,
            shared_send.at[index, kind],
            shared_arrive.at[index, kind],
            across if kind == 0 else near,
        )

    def shared_local(index):
        held, full = shared[index]
        return pltpu.make_async_copy(held, shared_rows(full, shard), local_sems.at[len(chunks) + index])

    def grad_copy(step):
        return add_remote(
            sent_grads.at[step],
            grads_out.at[me],
            grad_send.at[step],
            grad_arrive.at[step],
            device_of(paired(me, step, members)),
        )

    own_grads = pltpu.make_async_copy(sent_grads.at[0], grads_out.at[me], grad_send.at[0])

    def start_distant(index):
        @pl.when(native_here)
        def _():
            distant_copy(index, slot(index, 0)).start()

        @pl.when(jnp.logical_not(native_here))
        def _():
            distant_copy(index, passing(index)).start()

    def pass_on(index):
        @pl.when(native_here)
        def _():
            distant_copy(index, passing(index)).wait_recv()
            across_copy(index, passing(index)).start()
            near_copy(index, 0, piece(index)).start()

        @pl.when(jnp.logical_not(native_here))
        def _():
            distant_copy(index, slot(index, 0)).wait_recv()
            near_copy(index, 0, slot(index, 0)).start()

    def finish(index):
        across_copy(index, passing(index)).wait_recv()
        near_copy(index, 1, slot(index, 1)).start()

    def held_rows(member):
        places = lax.broadcasted_iota(jnp.int32, (capacity, tokens), 0).astype(f32)
        return (counts[pl.ds(member, 1), :] == places).astype(bf16)

    barrier = pltpu.get_barrier_semaphore()
    for device in (across, near, distant):
        pl.semaphore_signal(barrier, inc=1, device_id=device, device_id_type=mesh_ids)

    @pl.loop(1, members)
    def _(step):
        device = device_of(paired(me, step, members))
        pl.semaphore_signal(barrier, inc=1, device_id=device, device_id_type=mesh_ids)

    for index in range(2):
        shared_local(index).start()

    @pl.when(native_here)
    def _():
        for index in chunks:
            local_copy(index).start()

    pl.semaphore_wait(barrier, members + 2)
    shared_copy(0, 0).start()
    shared_copy(0, 1).start()
    for index in range(3):
        start_distant(index)
    shared_copy(1, 0).start()
    shared_copy(1, 1).start()

    tile_rows = tile

    @pl.loop(0, tokens // tile_rows)
    def _(part):
        rows = pl.ds(pl.multiple_of(part * tile_rows, tile_rows), tile_rows)
        values = residual_ref[rows, :]
        scale = lax.rsqrt(jnp.mean(values * values, axis=1, keepdims=True) + epsilon)
        normed[rows, :] = (values * scale * gains_ref[:1, :]).astype(bf16)
        low_grads[rows, :] = out_grad_ref[rows, :].astype(bf16)

    names = lax.broadcasted_iota(jnp.int32, (members, tokens), 0)
    member = (route_rows[:1, :] == names) | (route_rows[1:, :] == names)
    earlier = lax.broadcasted_iota(jnp.int32, (tokens, tokens), 0) < lax.broadcasted_iota(
        jnp.int32, (tokens, tokens), 1
    )
    ranks = dot_nn(member.astype(bf16), earlier.astype(bf16))
    counts[...] = jnp.where(member, ranks, -1.0)

    @pl.loop(0, members)
    def _(step):
        block = dot_nn(held_rows(paired(me, step, members)), low_grads[...])
        sent_grads[step] = block.astype(bf16)

    shared_copy(0, 0).wait_recv()
    shared_copy(0, 2).start()
    own_grads.start()

    @pl.loop(1, members)
    def _(step):
        grad_copy(step).start()

    column = turned_row(row_ref[...])
    for start_row in range(0, tokens, tile):
        start = key_start(start_row)
        span_width = start_row + tile - start
        others = row_ref[:, start : start_row + tile].astype(f32)
        same = column[start_row : start_row + tile, :1] == others
        ahead = lax.broadcasted_iota(jnp.int32, (tile, span_width), 1) - (start_row - start)
        later = ahead > lax.broadcasted_iota(jnp.int32, (tile, span_width), 0)
        mask_ref[start_row : start_row + tile, :span_width] = jnp.where(
            same & jnp.logical_not(later), 0.0, masked
        )
    logs[...] = jnp.zeros_like(logs)
    shared_local(0).wait()
    shared_copy(0, 1).wait_recv()
    shared_copy(0, 2).wait_recv()

    @pl.loop(0, 3 * width // tile)
    def _(part):
        columns = pl.ds(pl.multiple_of(part * tile, tile), tile)
        projected[:, columns] = dot_nn(normed[...], projection_full[:, columns]).astype(bf16)

    @pl.when(jnp.logical_not(native_here))
    def _():
        for index in chunks:
            across_copy(index, piece(index)).start()

    shared_copy(1, 0).wait_recv()
    shared_copy(1, 2).start()
    outs = (
        (projection_full, projection_out),
        (attended_full, attended_out),
        (projected, projected_out),
        (merged, merged_out),
        (logs, logs_out),
        (hidden, hidden_out),
        (normed, normed_out),
        (normed2, normed2_out),
        (counts, counts_out),
        (sent, sent_out),
        (gate_rows, gates_out),
    )

    def keep(index):
        return pltpu.make_async_copy(*outs[index], out_sems.at[index])

    for index in (0, 2, 6, 8):
        keep(index).start()
    pairs = width // lanes

    def attend(first_pair, last_pair):
        @pl.loop(first_pair, last_pair)
        def _(pair):
            columns = [
                pl.ds(pl.multiple_of(group * width + pair * lanes, lanes), lanes)
                for group in range(3)
            ]
            attend_forward_pair(
                head_dim,
                pair,
                projected.at[:, columns[0]],
                projected.at[:, columns[1]],
                projected.at[:, columns[2]],
                base_ref.at[pair],
                merged.at[:, columns[0]],
                logs,
                mask_ref,
            )

    attend(0, pairs // 2)
    for index in range(2):
        pass_on(index)
        start_distant(index + 3)
    attend(pairs // 2, pairs)
    shared_local(1).wait()
    shared_copy(1, 1).wait_recv()
    shared_copy(1, 2).wait_recv()
    for index in (1, 3, 4):
        keep(index).start()

    @pl.loop(0, width // tile)
    def _(part):
        columns = pl.ds(pl.multiple_of(part * tile, tile), tile)
        hidden[:, columns] = residual_ref[:, columns] + dot_nn(
            merged[...], attended_full[:, columns]
        )

    for index in range(2, 4):
        pass_on(index)
        start_distant(index + 3)
    keep(5).start()

    @pl.loop(0, tokens // tile_rows)
    def _(part):
        rows = pl.ds(pl.multiple_of(part * tile_rows, tile_rows), tile_rows)
        values = hidden[rows, :]
        scale = lax.rsqrt(jnp.mean(values * values, axis=1, keepdims=True) + epsilon)
        normed2[rows, :] = (values * scale * gains_ref[1:, :]).astype(bf16)

    keep(7).start()

    logits = dot_nt(router_ref[...], normed2[...])
    first, second = route_rows[:1, :] == names, route_rows[1:, :] == names
    lean = jnp.sum(jnp.where(first, logits, 0.0), axis=0, keepdims=True)
    lean = lean - jnp.sum(jnp.where(second, logits, 0.0), axis=0, keepdims=True)
    gate_table[...] = jnp.where(first, jax.nn.sigmoid(lean), 0.0) + jnp.where(
        second, jax.nn.sigmoid(-lean), 0.0
    )
    gate_rows[...] = jnp.zeros_like(gate_rows)

    @pl.loop(0, members)
    def _(member_index):
        held = held_rows(member_index)
        sent[member_index] = dot_nn(held, normed2[...]).astype(bf16)
        digits = split_digits(gate_table[pl.ds(member_index, 1), :])
        sums = jnp.sum(dot_nt(digits, held), axis=0, keepdims=True)
        gate_rows[member_index, :1, :capacity] = sums

    keep(9).start()
    keep(10).start()
    for index in range(4):
        finish(index)
    for index in range(4, 8):
        pass_on(index)
        if index + 3 < len(chunks):
            start_distant(index + 3)
        if index > 4:
            finish(index - 1)
    finish(len(chunks) - 1)

    own_grads.wait()

    @pl.loop(1, members)
    def _(step):
        grad_copy(step).wait()

    for index in range(len(outs)):
        keep(index).wait()
    for index in range(2):
        for kind in range(3):
            shared_copy(index, kind).wait_send()
    for index in chunks:
        distant_copy(index, passing(index)).wait_send()
        across_copy(index, passing(index)).wait_send()
        for which in range(2):
            near_copy(index, which, slot(index, which)).wait()

    @pl.when(native_here)
    def _():
        for index in chunks:
            local_copy(index).wait()


def run_front(
    residual_in,
    gains,
    projection_piece,
    attended_piece,
    inner_piece,
    outer_piece,
    route_rows,
    out_grad,
    marks,
    base_rows,
    router_turned,
    capacity,
    members,
    shards,
):
    tokens, width = residual_in.shape
    wide = projection_piece.shape[1]
    heads = base_rows.shape[0]
    pairs = width // lanes
    units = outer_piece.shape[0]
    whole = pl.BlockSpec(memory_space=pltpu.VMEM)
    anywhere = pl.BlockSpec(memory_space=pl.ANY)
    shape = jax.ShapeDtypeStruct
    held = [
        ((shards * projection_piece.shape[0], wide), bf16),
        ((shards * attended_piece.shape[0], width), bf16),
        ((tokens, wide), bf16),
        ((tokens, width), bf16),
        ((tokens, lanes), f32),
        ((tokens, width), f32),
        ((tokens, width), bf16),
        ((tokens, width), bf16),
        ((members, tokens), f32),
        ((members, capacity, width), bf16),
        ((members, 8, -(-capacity // lanes) * lanes), f32),
    ]
    dma = pltpu.SemaphoreType.DMA
    return pl.pallas_call(
        functools.partial(front_kernel, shards, width // heads),
        in_specs=[whole] * 2 + [anywhere] * 4 + [whole] * 5,
        out_specs=[anywhere] * 14,
        out_shape=[shape(*entry) for entry in held]
        + [
            shape((members, capacity, width), bf16),
            shape((width, shards * units), bf16),
            shape((shards * units, width), bf16),
        ],
        scratch_shapes=[pltpu.VMEM(*entry) for entry in held]
        + [
            pltpu.VMEM((members, capacity, width), bf16),
            pltpu.VMEM((tokens, width), bf16),
            pltpu.VMEM((tokens, span), f32),
            pltpu.VMEM((members, tokens), f32),
            pltpu.VMEM((2, units, width), bf16),
            dma((len(held),)),
            dma((10,)),
            dma((2, 3)),
            dma((2, 3)),
            dma((members,)),
            dma((members,)),
            dma((8,)),
            dma((8,)),
            dma((8,)),
            dma((8,)),
            dma((8, 2)),
            dma((8, 2)),
        ],
        compiler_params=pltpu.CompilerParams(
            collective_id=2, has_side_effects=True, vmem_limit_bytes=60 * 2**20
        ),
        cost_estimate=pl.CostEstimate(
            flops=2 * tokens * width * (wide + width) + 4 * members * capacity * tokens * width,
            bytes_accessed=20 * tokens * width,
            transcendentals=heads * tokens * tokens // 2,
        ),
    )(
        residual_in,
        gains,
        projection_piece,
        attended_piece,
        inner_piece,
        outer_piece,
        route_rows,
        out_grad,
        marks[None, :],
        base_rows.reshape(pairs, heads // pairs, span),
        router_turned,
    )


def held_tile(counts, capacity):
    places = lax.broadcasted_iota(jnp.int32, (capacity, counts.shape[1]), 0).astype(f32)
    blocks = [
        (counts[member : member + 1, :] == places).astype(bf16)
        for member in range(counts.shape[0])
    ]
    return jnp.concatenate(blocks, axis=0)


def row_scale(values):
    return lax.rsqrt(jnp.mean(values * values, axis=1, keepdims=True) + epsilon)


def back_kernel(
    shards,
    members,
    head_dim,
    capacity,
    reduce_here,
    logs,
    row_ref,
    route_rows,
    base_ref,
    normed2,
    merged,
    attended_full,
    router_ref,
    gains_ref,
    counts_ref,
    gates_back,
    projected_ref,
    normed_ref,
    projection_ref,
    back_ref,
    out_grad_ref,
    gated_ref,
    residual_ref,
    hidden_ref,
    inner_mine,
    inner_crossed,
    outer_mine,
    outer_given,
    inner_distant,
    residual_out,
    block_out,
    projection_out,
    attended_out,
    small_out,
    inner_final,
    outer_final,
    distant_in,
    outer_crossed,
    hidden_grad_ref,
    projected,
    normed,
    projection_full,
    mask_ref,
    log_turned,
    dk_total,
    dv_total,
    diagonal,
    grads,
    merged_grad,
    attended_grad,
    attended_part,
    bias_rows,
    parts,
    first_in,
    second_in,
    results_tile,
    results_ref,
    near_in,
    far_in,
    halves,
    half_in,
    quads,
    quad_in,
    pieces,
    piece_in,
    finished,
    finished_in,
    quad_back,
    half_back,
    small_own,
    small_in,
    small_sum,
    stream_sems,
    distant_sems,
    across_sems,
    outer_sems,
    near_sems,
    far_sems,
    half_sems,
    back_sems,
    quad_sems,
    piece_sems,
    finished_sems,
    quad_back_sems,
    small_sems,
    result_send,
    result_arrive,
    back_load_sems,
    final_sems,
    held_sems,
):
    tokens, width = normed2.shape
    pairs = width // lanes
    group = width // shards
    expert, shard = lax.axis_index("expert"), lax.axis_index("shard")
    side, half = shards // 2, members // 2
    low, turn = lax.rem(shard, side), shard // side
    native_here = expert // half == turn
    across = {"shard": lax.rem(shard + side, shards)}
    near = {"shard": turn * side + lax.rem(low + 1, side)}
    distant = {"expert": lax.rem(expert + half, members)}
    odd, level = lax.rem(expert, 2), expert // 2
    beside = {"expert": expert + 1 - 2 * odd}
    low_level, top_level = lax.rem(level, 2), level // 2
    above = {"expert": (level + 1 - 2 * low_level) * 2 + odd}
    high, wide = group // 4, width // 2
    own_columns = pl.ds(pl.multiple_of(top_level * wide, lanes), wide)
    other_columns = pl.ds(pl.multiple_of((1 - top_level) * wide, lanes), wide)

    def inner_remote(source):
        middle = width // 2
        return add_remote(
            source.at[middle:, :],
            distant_in.at[0, middle:, :],
            distant_sems.at[0],
            distant_sems.at[1],
            distant,
        )

    lines_each = width // 4

    def lines_of(index):
        return slice(index * lines_each, (index + 1) * lines_each)

    def across_copy(index):
        return add_remote(
            outer_given.at[lines_of(index), :],
            outer_crossed.at[lines_of(index), :],
            across_sems.at[0, index],
            across_sems.at[1, index],
            across,
        )

    def outer_distant(index, source):
        return add_remote(
            source.at[lines_of(index), :],
            distant_in.at[1, lines_of(index), :],
            outer_sems.at[0, index],
            outer_sems.at[1, index],
            distant,
        )

    def pass_outer(indices):
        @pl.when(native_here)
        def _():
            for index in indices:
                across_copy(index).wait_recv()
                outer_distant(index, outer_crossed).start()

    part_refs = [attended_part] + [parts.at[index] for index in range(3)]
    half_width = width // 2
    part_halves = [((0, 0), (1, 0)), ((2, 0), (0, 1)), ((1, 1), (2, 1))]
    me, device_of = group_place(members, shards)

    def result_rows():
        start = pl.multiple_of(me * capacity, 16)
        return results_ref.at[pl.ds(start, capacity), :]

    def result_copy(step):
        member = paired(me, step, members)
        return add_remote(
            gated_ref.at[member],
            result_rows(),
            result_send.at[step],
            result_arrive.at[step],
            device_of(member),
        )

    own_result = pltpu.make_async_copy(gated_ref.at[me], result_rows(), result_send.at[0])
    count = len(part_refs)

    def near_copy(index, top):
        start = pl.multiple_of((2 * top + 1 - low) * group, group)
        return add_remote(
            part_refs[index].at[pl.ds(start, group), :],
            near_in.at[index, top],
            near_sems.at[0, index, top],
            near_sems.at[1, index, top],
            near,
        )

    def far_copy(index):
        return add_remote(
            near_in.at[index, 1 - turn],
            far_in.at[index],
            far_sems.at[0, index],
            far_sems.at[1, index],
            across,
        )

    def half_copy(index):
        return add_remote(
            halves.at[index, 1 - odd],
            half_in.at[index],
            half_sems.at[0, index],
            half_sems.at[1, index],
            beside,
        )

    def quad_copy(index):
        return add_remote(
            quads.at[index, 1 - low_level],
            quad_in.at[index],
            quad_sems.at[0, index],
            quad_sems.at[1, index],
            above,
        )

    def piece_copy(index):
        return add_remote(
            pieces.at[index, 1 - top_level],
            piece_in.at[index],
            piece_sems.at[0, index],
            piece_sems.at[1, index],
            distant,
        )

    def finished_copy(index):
        return add_remote(
            finished.at[index],
            finished_in.at[index],
            finished_sems.at[0, index],
            finished_sems.at[1, index],
            distant,
        )

    def quad_back_copy(index):
        return add_remote(
            quads.at[index, low_level],
            quad_back.at[index],
            quad_back_sems.at[0, index],
            quad_back_sems.at[1, index],
            above,
        )

    def back_copy(index):
        return add_remote(
            halves.at[index, odd],
            half_back.at[index],
            back_sems.at[0, index],
            back_sems.at[1, index],
            beside,
        )

    def small_copy(stage):
        return add_remote(
            small_own if stage == 0 else small_sum.at[stage - 1],
            small_in.at[stage],
            small_sems.at[0, stage],
            small_sems.at[1, stage],
            (near, across, beside, above, distant)[stage],
        )

    def start_near(index):
        if reduce_here:
            for top in range(2):
                near_copy(index, top).start()

    def near_to_far(index):
        if reduce_here:
            for top in range(2):
                near_copy(index, top).wait_recv()
                start = pl.multiple_of((2 * top + low) * group, group)
                own = part_refs[index][pl.ds(start, group), :].astype(f32)
                near_in[index, top] = (own + near_in[index, top].astype(f32)).astype(bf16)
            far_copy(index).start()

    def far_to_half(index):
        if reduce_here:
            far_copy(index).wait_recv()
            total = near_in[index, turn].astype(f32) + far_in[index].astype(f32)
            total = total.astype(bf16)
            for place in range(2):
                halves[index, place] = total[2 * place * high : 2 * (place + 1) * high, :]
            half_copy(index).start()

    def half_to_quad(index):
        if reduce_here:
            half_copy(index).wait_recv()
            total = halves[index, odd].astype(f32) + half_in[index].astype(f32)
            total = total.astype(bf16)
            for place in range(2):
                quads[index, place] = total[place * high : (place + 1) * high, :]
            quad_copy(index).start()

    def quad_to_piece(index):
        if reduce_here:
            quad_copy(index).wait_recv()
            total = quads[index, low_level].astype(f32) + quad_in[index].astype(f32)
            total = total.astype(bf16)
            for place in range(2):
                pieces[index, place] = total[:, place * wide : (place + 1) * wide]
            piece_copy(index).start()

    def piece_to_finished(index):
        if reduce_here:
            piece_copy(index).wait_recv()
            total = pieces[index, top_level].astype(f32) + piece_in[index].astype(f32)
            finished[index] = total.astype(bf16)
            finished_copy(index).start()

    def finished_to_quad(index):
        if reduce_here:
            finished_copy(index).wait_recv()
            quads[index, low_level, :, own_columns] = finished[index]
            quads[index, low_level, :, other_columns] = finished_in[index]
            quad_back_copy(index).start()

    def quad_to_back(index):
        if reduce_here:
            quad_back_copy(index).wait_recv()
            own = pl.ds(pl.multiple_of(low_level * high, 16), high)
            other = pl.ds(pl.multiple_of((1 - low_level) * high, 16), high)
            halves[index, odd, own, :] = quads[index, low_level]
            halves[index, odd, other, :] = quad_back[index]
            back_copy(index).start()

    def write_out(index):
        if reduce_here:
            back_copy(index).wait_recv()
            for place, block in ((odd, halves.at[index, odd]), (1 - odd, half_back.at[index])):
                rows = pl.ds(pl.multiple_of(place * 2 * high, 2 * high), 2 * high)
                values = block[...].astype(f32)
                if index == 0:
                    attended_out[rows, :] = values
                else:
                    for place, (kind, side_of) in enumerate(part_halves[index - 1]):
                        left = kind * width + side_of * half_width
                        projection_out[rows, left : left + half_width] = values[
                            :, place * half_width : (place + 1) * half_width
                        ]

    def small_step(stage):
        if reduce_here:
            small_copy(stage).wait_recv()
            own = small_own[...] if stage == 0 else small_sum[stage - 1]
            small_sum[stage] = own + small_in[stage]
            if stage < 4:
                small_copy(stage + 1).start()

    held_loads = [
        pltpu.make_async_copy(source, target, held_sems.at[index])
        for index, (source, target) in enumerate(
            [(projected_ref, projected), (normed_ref, normed), (projection_ref, projection_full)]
        )
    ]
    barrier = pltpu.get_barrier_semaphore()
    partners = [across, distant]
    if reduce_here:
        partners = [across, near, beside, above, distant]
    for device in partners:
        pl.semaphore_signal(barrier, inc=1, device_id=device, device_id_type=mesh_ids)

    @pl.loop(1, members)
    def _(step):
        device = device_of(paired(me, step, members))
        pl.semaphore_signal(barrier, inc=1, device_id=device, device_id_type=mesh_ids)

    own_result.start()
    pl.semaphore_wait(barrier, len(partners) + members - 1)

    for index in range(4):
        across_copy(index).start()

    @pl.when(native_here)
    def _():
        inner_remote(inner_crossed).start()

    @pl.when(jnp.logical_not(native_here))
    def _():
        inner_remote(inner_mine).start()
        for index in range(4):
            outer_distant(index, outer_mine).start()

    def load_rows(source, target, part, kind):
        return pltpu.make_async_copy(
            source.at[part * tile : (part + 1) * tile, :],
            target.at[part % 2],
            stream_sems.at[kind, part % 2],
        )

    def store_rows(target, part):
        return pltpu.make_async_copy(
            results_tile.at[part % 2],
            target.at[part * tile : (part + 1) * tile, :],
            stream_sems.at[2, part % 2],
        )

    row_parts = tokens // tile
    back_count = members * capacity
    back_loads = [
        pltpu.make_async_copy(
            back_ref.at[top : min(top + tokens, back_count), :],
            grads.at[top // tokens, : min(tokens, back_count - top), :],
            back_load_sems.at[top // tokens],
        )
        for top in range(0, back_count, tokens)
    ]
    for copy in back_loads + held_loads:
        copy.start()
    for part in range(2):
        load_rows(hidden_ref, first_in, part, 0).start()
        load_rows(out_grad_ref, second_in, part, 1).start()

    log_turned[...] = logs[...].T
    column = turned_row(row_ref[...])
    for first in range(0, tokens, tile):
        start = key_start(first)
        span_width = first + tile - start
        own_marks = row_ref[:, first : first + tile].astype(f32)
        same = column[start : first + tile, :1] == own_marks
        ahead = lax.broadcasted_iota(jnp.int32, (span_width, tile), 0) - (first - start)
        later = ahead > lax.broadcasted_iota(jnp.int32, (span_width, tile), 1)
        mask_ref[:span_width, first : first + tile] = jnp.where(
            same & jnp.logical_not(later), 0.0, masked
        )
    small_own[...] = jnp.zeros_like(small_own)
    bias_top = small_own.shape[0] - pairs * bias_rows.shape[1]
    lane = lax.broadcasted_iota(jnp.int32, (tile, members), 1).astype(f32)
    for copy in back_loads:
        copy.wait()

    def middle_rows(part):
        rows = slice(part * tile, (part + 1) * tile)
        held = held_tile(counts_ref[:, rows], capacity)
        combined = functools.reduce(
            jnp.add,
            [
                dot_tn(
                    held[top : min(top + tokens, back_count), :],
                    grads[top // tokens, : min(tokens, back_count - top), :],
                )
                for top in range(0, back_count, tokens)
            ],
        )
        first, second = route_rows[:1, rows], route_rows[1:, rows]
        difference = jnp.zeros((1, tile), f32)
        for member in range(members):
            digits = split_digits(gates_back[member, :1, :capacity])
            sums = dot_nn(digits, held[member * capacity : (member + 1) * capacity, :])
            sums = jnp.sum(sums, axis=0, keepdims=True)
            difference = difference + jnp.where(jnp.minimum(first, second) == member, sums, -sums)
        difference = turned_row(difference)[:, :1]
        first, second = turned_row(first)[:, :1], turned_row(second)[:, :1]
        least, most = jnp.minimum(first, second), jnp.maximum(first, second)
        signs = (lane == least).astype(f32) - (lane == most).astype(f32)
        values = normed2[rows, :]
        lean = jnp.sum(dot_nt(values, router_ref[...]) * signs, axis=1, keepdims=True)
        gates = jax.nn.sigmoid(lean)
        logit_grad = gates * (1.0 - gates) * difference * signs
        above = logit_grad.astype(bf16)
        below = (logit_grad - above.astype(f32)).astype(bf16)
        router_grad = dot_tn(above, values) + dot_tn(below, values)
        small_own[2 : 2 + members, :] += router_grad
        gradient = dot_nn(above, router_ref[...]) + dot_nn(below, router_ref[...]) + combined
        load_rows(hidden_ref, first_in, part, 0).wait()
        load_rows(out_grad_ref, second_in, part, 1).wait()
        hidden = first_in[part % 2]
        scale = row_scale(hidden)
        weighted = gradient * gains_ref[1:, :]
        inner = jnp.mean(weighted * hidden, axis=1, keepdims=True)
        small_own[1:2, :] += jnp.sum(gradient * hidden * scale, axis=0, keepdims=True)
        if part >= 2:
            store_rows(hidden_grad_ref, part - 2).wait()
        hidden_grad = (
            second_in[part % 2] + scale * weighted - hidden * (scale * scale * scale * inner)
        )
        results_tile[part % 2] = hidden_grad
        store_rows(hidden_grad_ref, part).start()
        if part + 2 < row_parts:
            load_rows(hidden_ref, first_in, part + 2, 0).start()
            load_rows(out_grad_ref, second_in, part + 2, 1).start()
        low_grad = hidden_grad.astype(bf16)
        attended_grad[rows, :] = low_grad
        merged_grad[rows, :] = dot_nt(low_grad, attended_full[...]).astype(bf16)

    for part in range(row_parts):
        middle_rows(part)

    @pl.loop(0, width // tile)
    def _(part):
        columns = pl.ds(pl.multiple_of(part * tile, tile), tile)
        attended_part[:, columns] = dot_tn(merged[...], attended_grad[:, columns]).astype(bf16)

    start_near(0)
    for part in range(row_parts - 2, row_parts):
        store_rows(hidden_grad_ref, part).wait()

    def attend(first_pair, last_pair):
        @pl.loop(first_pair, last_pair)
        def _(pair):
            columns = [
                pl.ds(pl.multiple_of(place * width + pair * lanes, lanes), lanes)
                for place in range(3)
            ]
            own = columns[0]
            attend_backward_pair(
                head_dim,
                pair,
                projected.at[:, columns[0]],
                projected.at[:, columns[1]],
                projected.at[:, columns[2]],
                merged_grad.at[:, own],
                base_ref.at[pair],
                grads.at[0, :, own],
                grads.at[1, :, own],
                grads.at[2, :, own],
                bias_rows.at[pair],
                mask_ref,
                log_turned,
                dk_total,
                dv_total,
                diagonal,
            )

    @pl.loop(1, members)
    def _(step):
        result_copy(step).start()

    def make_part(index):
        for place, (kind, side_of) in enumerate(part_halves[index]):
            left = side_of * half_width
            sums = dot_tn(normed[...], grads[kind, :, left : left + half_width])
            parts[index, :, place * half_width : (place + 1) * half_width] = sums.astype(bf16)
        start_near(index + 1)

    for copy in held_loads:
        copy.wait()
    pass_outer(range(2))
    attend(0, 1)
    pass_outer(range(2, 4))
    attend(1, pairs // 2)
    make_part(0)
    near_to_far(0)

    attend(pairs // 2, pairs)
    far_to_half(0)
    near_to_far(1)
    for index in range(1, 3):
        make_part(index)
    per_pair = bias_rows.shape[1]
    for pair in range(pairs):
        top = bias_top + pair * per_pair
        small_own[top : top + per_pair, :] = bias_rows[pair]

    def norm_rows(part):
        rows = slice(part * tile, (part + 1) * tile)
        normed_grad = functools.reduce(
            jnp.add,
            [
                dot_nt(grads[index, rows, :], projection_full[:, index * width : (index + 1) * width])
                for index in range(3)
            ],
        )
        load_rows(residual_ref, first_in, part, 0).wait()
        load_rows(hidden_grad_ref, second_in, part, 1).wait()
        values = first_in[part % 2]
        scale = row_scale(values)
        weighted = normed_grad * gains_ref[:1, :]
        inner = jnp.mean(weighted * values, axis=1, keepdims=True)
        if part >= 2:
            store_rows(residual_out, part - 2).wait()
        results_tile[part % 2] = (
            second_in[part % 2] + scale * weighted - values * (scale * scale * scale * inner)
        )
        small_own[:1, :] += jnp.sum(normed_grad * values * scale, axis=0, keepdims=True)
        store_rows(residual_out, part).start()
        if part + 2 < tokens // tile:
            load_rows(residual_ref, first_in, part + 2, 0).start()
            load_rows(hidden_grad_ref, second_in, part + 2, 1).start()
        else:
            load_rows(hidden_ref, first_in, part % 2, 0).start()

    def block_rows(part):
        held = held_tile(counts_ref[:, part * tile : (part + 1) * tile], capacity)
        sums = dot_tn(held, results_ref[...])
        load_rows(hidden_ref, first_in, part, 0).wait()
        if part < 2:
            store_rows(residual_out, tokens // tile - 2 + part).wait()
        else:
            store_rows(block_out, part - 2).wait()
        results_tile[part % 2] = first_in[part % 2] + sums
        store_rows(block_out, part).start()
        if part + 2 < tokens // tile:
            load_rows(hidden_ref, first_in, part + 2, 0).start()

    def final_load(matrix, source, kind):
        target = (attended_grad, merged_grad)[kind]
        return pltpu.make_async_copy(source, target.at[:width, :], final_sems.at[matrix, kind])

    def start_final(matrix):
        mine, crossed = ((inner_mine, inner_crossed), (outer_mine, outer_crossed))[matrix]

        @pl.when(native_here)
        def _():
            final_load(matrix, mine, 0).start()

        @pl.when(jnp.logical_not(native_here))
        def _():
            if matrix == 1:
                for index in range(4):
                    across_copy(index).wait_recv()
            final_load(matrix, crossed, 0).start()

        if matrix == 0:
            inner_remote(inner_mine).wait_recv()
        else:
            for index in range(4):
                outer_distant(index, outer_mine).wait_recv()
        for copy in distant_loads(matrix):
            copy.start()

    def distant_loads(matrix):
        middle = width // 2
        if matrix == 1:
            return [final_load(1, distant_in.at[1], 1)]
        return [
            pltpu.make_async_copy(
                inner_distant, merged_grad.at[:middle, :], final_sems.at[0, 1]
            ),
            pltpu.make_async_copy(
                distant_in.at[0, middle:, :],
                merged_grad.at[middle:width, :],
                final_sems.at[1, 3],
            ),
        ]

    final_stores = [
        pltpu.make_async_copy(
            diagonal.at[0], inner_final.at[: 2 * tile, :], final_sems.at[0, 2]
        ),
        pltpu.make_async_copy(
            diagonal.at[1, :tile, :], inner_final.at[2 * tile :, :], final_sems.at[0, 3]
        ),
        pltpu.make_async_copy(mask_ref.at[:, :width], outer_final, final_sems.at[1, 2]),
    ]

    def finish_final(matrix):
        for copy in [final_load(matrix, inner_mine, 0)] + distant_loads(matrix):
            copy.wait()
        for part in range(3):
            lines = slice(part * tile, (part + 1) * tile)
            sums = attended_grad[lines, :].astype(f32) + merged_grad[lines, :].astype(f32)
            if matrix == 1:
                mask_ref[:, lines] = sums.T
            else:
                diagonal[part // 2, part % 2 * tile : (part % 2 + 1) * tile, :] = sums
        for copy in final_stores[2:] if matrix == 1 else final_stores[:2]:
            copy.start()

    for part in range(2):
        load_rows(residual_ref, first_in, part, 0).start()
        load_rows(hidden_grad_ref, second_in, part, 1).start()
    half_to_quad(0)
    for index in range(2, count):
        near_to_far(index)
    far_to_half(1)
    norm_rows(0)
    quad_to_piece(0)
    half_to_quad(1)
    norm_rows(1)
    for index in range(2, count):
        far_to_half(index)
    piece_to_finished(0)
    quad_to_piece(1)
    norm_rows(2)
    for index in range(2, count):
        half_to_quad(index)
    finished_to_quad(0)
    piece_to_finished(1)
    for part in range(3, row_parts):
        norm_rows(part)
    if reduce_here:
        small_copy(0).start()
    for index in range(2, count):
        quad_to_piece(index)
    finished_to_quad(1)
    own_result.wait()

    @pl.loop(1, members)
    def _(step):
        result_copy(step).wait()

    block_rows(0)
    small_step(0)
    for index in range(2, count):
        piece_to_finished(index)
    for index in range(2):
        quad_to_back(index)
    block_rows(1)
    small_step(1)
    for index in range(2, count):
        finished_to_quad(index)
    start_final(0)
    block_rows(2)
    small_step(2)
    for index in range(2, count):
        quad_to_back(index)
    for part in range(3, row_parts):
        block_rows(part)
    small_step(3)
    finish_final(0)
    small_step(4)
    start_final(1)
    finish_final(1)
    for index in range(count):
        write_out(index)
    if reduce_here:
        small_out[...] = small_sum[4]
    else:
        small_out[...] = small_own[...]
        for index in range(3):
            for place, (kind, side_of) in enumerate(part_halves[index]):
                left = kind * width + side_of * half_width
                projection_out[:, left : left + half_width] = parts[
                    index, :, place * half_width : (place + 1) * half_width
                ]
        attended_out[...] = attended_part[...]

    for part in range(row_parts - 2, row_parts):
        store_rows(block_out, part).wait()
    inner_remote(inner_mine).wait_send()
    for index in range(4):
        across_copy(index).wait_send()
        outer_distant(index, outer_mine).wait_send()
    for copy in final_stores:
        copy.wait()
    if reduce_here:
        for index in range(count):
            for top in range(2):
                near_copy(index, top).wait_send()
            far_copy(index).wait_send()
            back_copy(index).wait_send()
            half_copy(index).wait_send()
            quad_copy(index).wait_send()
            piece_copy(index).wait_send()
            finished_copy(index).wait_send()
            quad_back_copy(index).wait_send()
        for stage in range(5):
            small_copy(stage).wait_send()


def run_back(
    projected,
    logs,
    marks,
    route_rows,
    base_turned,
    normed,
    normed2,
    merged,
    projection_full,
    attended_full,
    router,
    gains,
    counts,
    gates_back,
    back,
    out_grad,
    gated,
    residual_in,
    hidden,
    weights,
    capacity,
    members,
    shards,
):
    tokens, width = normed.shape
    heads = base_turned.shape[0]
    pairs = width // lanes
    per_pair = heads // pairs
    group = width // shards
    units = weights[0].shape[1]
    small_shape = (-(-(2 + members + heads) // 8) * 8, width)
    reduce_here = members == 8 and shards == 4 and group % 64 == 0 and width % 256 == 0
    high, wide = group // 4, width // 2
    whole = pl.BlockSpec(memory_space=pltpu.VMEM)
    anywhere = pl.BlockSpec(memory_space=pl.ANY)
    shape = jax.ShapeDtypeStruct
    if reduce_here:
        sums = [shape((group, 3 * width), f32), shape((group, width), f32)]
    else:
        sums = [shape((width, 3 * width), bf16), shape((width, width), bf16)]
        high, wide = 16, lanes
    count = 4
    dma = pltpu.SemaphoreType.DMA
    vmem = pltpu.VMEM
    piece = (count, high, wide)
    quad = (count, high, 2 * wide)
    outs = pl.pallas_call(
        functools.partial(
            back_kernel, shards, members, width // heads, capacity, reduce_here
        ),
        in_specs=[whole] * 11 + [anywhere] * 13,
        out_specs=[anywhere] * 2 + [whole] * 3 + [anywhere] * 5,
        out_shape=[shape((tokens, width), f32)] * 2
        + sums
        + [
            shape(small_shape, f32),
            shape((width, units), f32),
            shape((units, width), f32),
            shape((2, width, units), bf16),
            shape((width, units), bf16),
            shape((tokens, width), f32),
        ],
        scratch_shapes=[
            vmem(projected.shape, bf16),
            vmem(normed.shape, bf16),
            vmem(projection_full.shape, bf16),
            vmem((span, tokens), f32),
            vmem((lanes, tokens), f32),
            vmem((tokens, lanes), f32),
            vmem((tokens, lanes), f32),
            vmem((per_pair, 2 * tile, span), f32),
            vmem((3, tokens, width), bf16),
            vmem((tokens, width), bf16),
            vmem((tokens, width), bf16),
            vmem((width, width), bf16),
            vmem((pairs, per_pair, span), f32),
            vmem((3, width, width), bf16),
            vmem((2, tile, width), f32),
            vmem((2, tile, width), f32),
            vmem((2, tile, width), f32),
            vmem((members * capacity, width), bf16),
            vmem((count, 2, group, width), bf16),
            vmem((count, group, width), bf16),
            vmem((count, 2, 2 * high, 2 * wide), bf16),
            vmem((count, 2 * high, 2 * wide), bf16),
            vmem((count, 2, high, 2 * wide), bf16),
            vmem(quad, bf16),
            vmem((count, 2, high, wide), bf16),
            vmem(piece, bf16),
            vmem(piece, bf16),
            vmem(piece, bf16),
            vmem(quad, bf16),
            vmem((count, 2 * high, 2 * wide), bf16),
            vmem(small_shape, f32),
            vmem((5,) + small_shape, f32),
            vmem((5,) + small_shape, f32),
            dma((3, 2)),
            dma((2,)),
            dma((2, 4)),
            dma((2, 4)),
            dma((2, count, 2)),
            dma((2, count)),
            dma((2, count)),
            dma((2, count)),
            dma((2, count)),
            dma((2, count)),
            dma((2, count)),
            dma((2, count)),
            dma((2, 5)),
            dma((members,)),
            dma((members,)),
            dma((4,)),
            dma((2, 4)),
            dma((3,)),
        ],
        compiler_params=pltpu.CompilerParams(
            collective_id=4, has_side_effects=True, vmem_limit_bytes=62 * 2**20
        ),
        cost_estimate=pl.CostEstimate(
            flops=16 * tokens * tokens * width,
            bytes_accessed=40 * tokens * width,
            transcendentals=heads * tokens * tokens // 2,
        ),
    )(
        logs,
        marks[None, :],
        route_rows,
        base_turned.reshape(pairs, per_pair, span),
        normed2,
        merged,
        attended_full,
        router,
        gains,
        counts,
        gates_back,
        projected,
        normed,
        projection_full,
        back,
        out_grad,
        gated,
        residual_in,
        hidden,
        *weights,
    )
    return outs[:-3], reduce_here


def sum_rows(part):
    return lax.all_gather(
        lax.psum_scatter(part.astype(bf16), ("shard", "expert"), scatter_dimension=0, tiled=True),
        "expert",
        axis=0,
        tiled=True,
    ).astype(f32)


def per_device(
    residual_in,
    norm1_gain,
    w_projection,
    rel_bias,
    w_attn_out,
    norm2_gain,
    w_router,
    expert_in,
    expert_out,
    segments,
    routes,
    out_grad,
):
    highest = lax.Precision.HIGHEST
    tokens_here, width = residual_in.shape
    heads, buckets = rel_bias.shape
    experts_all = w_router.shape[1]
    capacity = -(-5 * tokens_here // (32 * experts_all)) * 16
    marks = segments.reshape(-1)
    experts = jnp.arange(experts_all, dtype=jnp.int32)
    table_rows, table_turned = bias_tables(buckets)

    gains = jnp.stack([norm1_gain, norm2_gain])
    router = w_router.T
    route_rows = routes.T
    base_rows = jnp.dot(rel_bias, table_rows.T, precision=highest)
    base_turned = jnp.dot(rel_bias, table_turned.T, precision=highest)
    (
        full_projection,
        full_attn_out,
        projected,
        merged,
        logs,
        hidden,
        normed,
        normed2,
        counts,
        sent,
        gate_rows,
        arrived_grad,
        inner,
        outer,
    ) = run_front(
        residual_in,
        gains,
        w_projection,
        w_attn_out,
        expert_in[0],
        expert_out[0],
        route_rows,
        out_grad,
        marks,
        base_rows,
        router,
        capacity,
        experts_all,
        lax.axis_size("shard"),
    )
    shards = lax.axis_size("shard")
    gated, back_rows, gates_back, *weights = run_experts(
        sent, gate_rows, arrived_grad, inner, outer, shards
    )
    inner_mine, outer_mine, outer_given, inner_crossed, inner_distant = weights
    filled = 2 + experts_all
    outs, reduced = run_back(
        projected,
        logs,
        marks,
        route_rows,
        base_turned,
        normed,
        normed2,
        merged,
        full_projection,
        full_attn_out,
        router,
        gains,
        counts,
        gates_back,
        back_rows.reshape(-1, width),
        out_grad,
        gated,
        residual_in,
        hidden,
        (inner_mine, inner_crossed, outer_mine, outer_given, inner_distant),
        capacity,
        experts_all,
        shards,
    )
    residual_grad, block_out, projection_total, attn_out_total, small = outs[:5]
    expert_in_grad, expert_out_grad = outs[5:]
    if not reduced:
        projection_total = sum_rows(projection_total)
        attn_out_total = sum_rows(attn_out_total)
        small = lax.psum(small, ("expert", "shard"))
    gain1_total, gain2_total = small[0], small[1]
    router_total = small[2:filled].T
    bias_total = jnp.dot(small[small.shape[0] - heads :], table_turned, precision=highest)
    return (
        block_out,
        residual_grad,
        gain1_total,
        projection_total,
        bias_total,
        attn_out_total,
        gain2_total,
        router_total,
        expert_in_grad[None],
        expert_out_grad[None],
    )


def solution(mesh):
    return jax.shard_map(
        per_device,
        mesh=mesh,
        in_specs=(
            P(("expert", "shard"), None),
            P(),
            P("shard", None),
            P(),
            P("shard", None),
            P(),
            P(),
            P("expert", None, "shard"),
            P("expert", "shard", None),
            P(("expert", "shard"), None),
            P(("expert", "shard"), None),
            P(("expert", "shard"), None),
        ),
        out_specs=(
            P(("expert", "shard"), None),
            P(("expert", "shard"), None),
            P(),
            P("shard", None),
            P(),
            P("shard", None),
            P(),
            P(),
            P("expert", None, "shard"),
            P("expert", "shard", None),
        ),
        check_vma=False,
    )
```
